32 devices in a mesh: graph: 16 (over z, y, x), mp: 2 (over core).
Axes of the slice: x: 2, y: 2, z: 4, core: 2. Of those that a mesh axis runs over, the one named last changes fastest.
Arguments:
- messages: bfloat16 [16384, 512], P('graph', 'mp'), may hold values from -6 to 6
- basis_blocks: bfloat16 [1536, 128, 128], P('graph'), may hold values from -0.5 to 0.5
- source_block: int32 [1536], P('graph'), may hold values from 0 to 7
- target_owner: int32 [1536, 1], P('graph'), may hold values from 0 to 15; in each aligned block of 96 rows (0 to 95, 96 to 191, ...) at most 7 rows name the same one
- target_block: int32 [1536], P('graph'), may hold values from 0 to 7
- row_counts: int32 [1536], P('graph'), may hold values from 1 to 128
- reverse_block: int32 [128], P('graph'), may hold values from 0 to 127, as said below
- valid_edges: int32 [16], P('graph'), may hold values from 512 to 1024
- weight_in: bfloat16 [3, 512, 512], P(None, None, 'mp'), may hold values from -0.25 to 0.25
- weight_out: bfloat16 [3, 512, 512], P(None, 'mp'), may hold values from -0.25 to 0.25
Outputs:
- updated: bfloat16 [16384, 512], P('graph', 'mp')
The draws below stay inside these ranges and needn't reach their ends.
Inputs may be any that keep to these rules, and one draw needn't show every extreme that they name: `target_owner`: among the 96 triplet blocks of one device, no owner is named more than 7 times, a bound that some block reaches. `reverse_block`: an involution on edge blocks. Of device g's 8 blocks, the first 2 pair with blocks 2 to 3 of device (g - 1) mod 16, blocks 2 to 3 pair with the first 2 of device (g + 1) mod 16, and the others pair with blocks of device g itself.
All inputs are finite; a program needn't handle non-finite values.
Results may differ from the reference program's by a relative error of at most 0.0073.
Values may be sent and summed in bfloat16 or wider, within the bound.
No kernel may reach another device: no remote copies, remote signals or barrier semaphores. Data moves between devices by JAX's collectives and lax.ppermute only.
A program may use at most 128 MiB of HBM per device.

```python
import math
import jax
import jax.numpy as jnp
import numpy as np
from jax import lax

H = 512
MLPS = 3
BLK = 128
E_DEV = 1024
SLOTS = 96
EB = 8
RB = 2
CAP = 7
EDGES = 16384
NBLOCKS = 128
SLOTS_ALL = 1536
N_GRAPH = 16


def draw_reverse_block(key, part):
    key_edge, key_inner = jax.random.split(jax.random.fold_in(key, 7))
    devices = jnp.arange(N_GRAPH, dtype=jnp.int32)
    inner_count = EB - 2 * RB

    def edge_order(device):
        return jax.random.permutation(jax.random.fold_in(key_edge, device), RB).astype(jnp.int32)

    def inner_order(device):
        return jax.random.permutation(jax.random.fold_in(key_inner, device), inner_count).astype(jnp.int32)
    edge_perm = jax.vmap(edge_order)(devices)
    edge_inverse = jnp.argsort(edge_perm, axis=1).astype(jnp.int32)
    inner_perm = jax.vmap(inner_order)(devices)
    swapped = inner_perm.reshape(N_GRAPH, inner_count // 2, 2)[:, :, ::-1].reshape(N_GRAPH, inner_count)
    partner = jnp.zeros((N_GRAPH, inner_count), jnp.int32).at[devices[:, None], inner_perm].set(swapped)
    previous = (devices - 1) % N_GRAPH
    following = (devices + 1) % N_GRAPH
    head = previous[:, None] * EB + RB + edge_perm
    second = following[:, None] * EB + edge_inverse[following]
    middle = devices[:, None] * EB + 2 * RB + partner
    return jnp.concatenate([head, second, middle], axis=1).reshape(-1).astype(jnp.int32)


def plant(values, stream_key, smallest, high):
    extent = values.shape
    place = [jax.random.randint(jax.random.fold_in(stream_key, axis), (), 0, extent[axis]) for axis in range(len(extent))]
    values = values.at[tuple(place)].set(smallest)
    longest = extent.index(max(extent))
    place[longest] = (place[longest] + 1) % extent[longest]
    return values.at[tuple(place)].set(high)


def levels(stream_key, extent, cuts, smallest, largest):
    factor_of = 1.0
    for dim, blocks in cuts:
        heights = jax.random.uniform(jax.random.fold_in(jax.random.fold_in(stream_key, 6), dim), (blocks,), jnp.float32, smallest / len(cuts), largest / len(cuts))
        factor_of = factor_of * jnp.repeat(jnp.exp(heights), extent[dim] // blocks).reshape((-1,) + (1,) * (len(extent) - 1 - dim))
    return factor_of


def routed_block(own_key, own, number, rows, amount, top, most, slope):
    order = jax.random.permutation(own_key, amount)
    crowded, ordinary = shares(amount, rows * top, most, slope, True), shares(amount, rows * top, most, slope, False)
    places = jnp.arange(amount)

    def named(sizes, rotation):
        used = int((sizes > 0).sum())
        fixed = max(1, used // 4)
        shifted = fixed + (places - fixed + rotation * (used - fixed)) % max(1, amount - fixed)
        return jnp.zeros((amount,), jnp.int32).at[order[jnp.where(places < fixed, places, shifted)]].set(jnp.asarray(sizes, jnp.int32))

    sizes = jnp.where(number % 4 == 0, named(crowded, number // 4), named(ordinary, number - number // 4 - 1))
    mixed = jax.random.permutation(jax.random.fold_in(own, 3), amount)
    giver, taker = mixed[0:amount // 2 * 2:2], mixed[1:amount // 2 * 2:2]
    slack = jnp.minimum(sizes[giver] - 1, most - sizes[taker]) // 2
    slack = jnp.where((giver == order[0]) | (taker == order[0]) | (sizes[taker] == 0), 0, jnp.maximum(slack, 0))
    shifted = jax.random.randint(jax.random.fold_in(own, 4), (amount // 2,), 0, 1 << 20) % (slack + 1)
    sizes = sizes.at[giver].add(-shifted).at[taker].add(shifted)
    labels = jnp.searchsorted(jnp.cumsum(sizes), jnp.arange(rows * top), side="right").astype(jnp.int32)
    grid = labels.reshape(top, rows).T
    grid = grid[jax.random.permutation(jax.random.fold_in(own, 1), rows)]
    rotation = jax.random.randint(jax.random.fold_in(own, 2), (rows, 1), 0, top)
    return jnp.take_along_axis(grid, (jnp.arange(top)[None, :] + rotation) % top, axis=1)


def shares(count, total, reach, lean, full):
    portions = [(1 << 20) // math.isqrt(rank ** lean) + 1 for rank in range(1, count + 1)]
    largest = reach if full else min(reach, max(-(-total // count), total * portions[0] // sum(portions)))
    least = 1 if total - largest >= count - 1 else 0
    given, rest = [largest] + [least] * (count - 1), total - largest - least * (count - 1)
    while rest > 0:
        movable = [i for i in range(1, count) if given[i] < largest] or [i for i in range(1, count) if given[i] < reach]
        whole, budget = sum([portions[i] for i in movable]), rest
        for i in movable:
            extra = min(reach - given[i], max(1, budget * portions[i] // whole), rest)
            given[i] = given[i] + extra
            rest = rest - extra
    return np.array(given)


def bell_draw(key, shape, deviation, bound, cuts=(), kind=jnp.bfloat16):
    gain = levels(key, shape, cuts, -0.22, 0.18) if cuts else 1.0
    values = jax.random.normal(key, shape, jnp.float32) * deviation * gain
    return jnp.minimum(jnp.maximum(values, -bound), bound).astype(kind)


def setup_inputs(seed: int = 0) -> dict:
    splits = jax.random.split(jax.random.key(seed), 11)
    messages = bell_draw(splits[0], (EDGES, H), 1.0, 6.0, ((0, 16), (1, 2)))
    basis_blocks = bell_draw(splits[1], (SLOTS_ALL, BLK, BLK), BLK ** -0.5, 0.5, ((0, 16),))
    source_block = plant(jax.random.randint(splits[2], (SLOTS_ALL,), 0, EB), jax.random.fold_in(splits[2], 1), 0, EB - 1).astype(jnp.int32)
    target_owner_keys = jax.random.split(jax.random.fold_in(splits[3], 1), SLOTS_ALL // SLOTS)
    target_owner_turns = jax.random.permutation(jax.random.fold_in(splits[3], 3), SLOTS_ALL // SLOTS)
    target_owner = jax.vmap(lambda own, number: routed_block(jax.random.fold_in(splits[3], 2), own, number, SLOTS, N_GRAPH, 1, CAP, 2))(target_owner_keys, target_owner_turns).reshape((SLOTS_ALL, 1))
    target_block = plant(jax.random.randint(splits[4], (SLOTS_ALL,), 0, EB), jax.random.fold_in(splits[4], 1), 0, EB - 1).astype(jnp.int32)
    row_counts = plant(jax.random.randint(splits[5], (SLOTS_ALL,), 1, BLK + 1), jax.random.fold_in(splits[5], 1), 1, BLK).astype(jnp.int32)
    reverse_block = draw_reverse_block(jax.random.fold_in(splits[10], 71), 0)
    valid_edges = plant(jax.random.randint(splits[7], (N_GRAPH,), E_DEV // 2, E_DEV + 1), jax.random.fold_in(splits[7], 1), E_DEV // 2, E_DEV).astype(jnp.int32)
    weight_in = bell_draw(splits[8], (MLPS, H, H), H ** -0.5, 0.25, ((2, 2),))
    weight_out = bell_draw(splits[9], (MLPS, H, H), H ** -0.5, 0.25, ((1, 2),))
    return dict(messages=messages, basis_blocks=basis_blocks, source_block=source_block, target_owner=target_owner, target_block=target_block, row_counts=row_counts, reverse_block=reverse_block, valid_edges=valid_edges, weight_in=weight_in, weight_out=weight_out)


pair_scale = 0.7071067811865476


def reference(messages, basis_blocks, source_block, target_owner, target_block, row_counts, reverse_block, valid_edges, weight_in, weight_out):
    block_view = messages.reshape(NBLOCKS, BLK, H)
    row_index = jnp.arange(BLK, dtype=jnp.int32)

    def per_device(total, inputs):
        device, basis, source, owner, target, counts = inputs
        gathered = block_view[(device * EB + source).astype(jnp.int32)]
        product = jnp.einsum('str,src->stc', basis.astype(jnp.float32), gathered.astype(jnp.float32))
        keep = row_index[None, :] < counts[:, None]
        product = jnp.where(keep[:, :, None], product, 0.0).astype(jnp.bfloat16)
        target_global = (owner * EB + target).astype(jnp.int32)
        total = total.at[target_global].add(product.astype(jnp.float32))
        return total, None

    scanned = (jnp.arange(N_GRAPH, dtype=jnp.int32),
               basis_blocks.reshape(N_GRAPH, SLOTS, BLK, BLK),
               source_block.reshape(N_GRAPH, SLOTS),
               target_owner[:, 0].reshape(N_GRAPH, SLOTS),
               target_block.reshape(N_GRAPH, SLOTS),
               row_counts.reshape(N_GRAPH, SLOTS))
    aggregate, _ = lax.scan(per_device, jnp.zeros((NBLOCKS, BLK, H), jnp.float32), scanned)
    combined = (block_view.astype(jnp.float32) + aggregate).astype(jnp.bfloat16)
    swapped = combined[reverse_block]
    state = ((combined.astype(jnp.float32) + swapped.astype(jnp.float32)) * pair_scale).reshape(EDGES, H)
    for layer in range(MLPS):
        layer_input = state.astype(jnp.bfloat16)
        hidden = jax.nn.silu(jnp.dot(layer_input, weight_in[layer], preferred_element_type=jnp.float32)).astype(jnp.bfloat16)
        state = state + jnp.dot(hidden, weight_out[layer], preferred_element_type=jnp.float32)
    position = jnp.arange(EDGES, dtype=jnp.int32)
    keep_edge = (position % E_DEV) < valid_edges[position // E_DEV]
    return jnp.where(keep_edge[:, None], state, 0.0).astype(jnp.bfloat16)
```

```python
import functools

import jax
import jax.numpy as jnp
from jax import lax
from jax.experimental import pallas as pl
from jax.experimental.pallas import tpu as pltpu
from jax.sharding import PartitionSpec as P

MLPS = 3
BLK = 128
CHUNKS = 2
UNROLL = 4
VMEM_LIMIT = 56 * 1024 * 1024

pair_scale = 0.7071067811865476


def split_bits(devices):
    count = devices.bit_length() - 1
    near = [bit for bit in (0, 2) if bit < count]
    far = [bit for bit in range(count) if bit not in near]
    return near, far


def xor_pairs(devices, mask):
    return [(i, i ^ mask) for i in range(devices)]


def near_mask(near, k):
    return sum(((k >> i) & 1) << bit for i, bit in enumerate(near))


def full(shape):
    return pl.BlockSpec(memory_space=pltpu.VMEM)


def smem():
    return pl.BlockSpec(memory_space=pltpu.SMEM)


def pack_kernel(near, far, room, rows, blocks, owner, source, target, counts, basis, *refs):
    groups = 1 << len(near)
    packed = [refs[k * CHUNKS : (k + 1) * CHUNKS] for k in range(groups)]
    metas = refs[groups * CHUNKS : groups * (CHUNKS + 1)]
    table, fill = refs[groups * (CHUNKS + 1) :]
    slots = basis.shape[0]
    me = lax.axis_index("graph")
    core = lax.axis_index("mp")
    for k in range(groups):
        fill[k] = 0

    def clear(i, carry):
        table[i] = -1
        return carry

    lax.fori_loop(0, groups * room, clear, 0)

    def route(t, carry):
        rel = owner[t] ^ me
        k = 0
        for i, bit in enumerate(near):
            k = k + (((rel >> bit) & 1) << i)
        p = fill[k]
        fill[k] = p + 1
        table[k * room + p] = t
        return carry

    lax.fori_loop(0, slots, route, 0)

    row = lax.broadcasted_iota(jnp.int32, (rows, BLK), 0)
    for k in range(groups):

        def one(p, carry):
            t = table[k * room + p]
            there = t >= 0
            s = jnp.maximum(t, 0)
            rel = owner[s] ^ me
            b = 0
            for i, bit in enumerate(far):
                b = b + (((rel >> bit) & 1) << (len(far) - 1 - i))
            label = (b * blocks + target[s]) * blocks + source[s]
            metas[k][p] = jnp.where(there, label, 0)
            count = jnp.where(there, counts[s], 0)
            for j in range(CHUNKS):
                first = core * (rows * CHUNKS) + j * rows
                block = basis[s, pl.ds(pl.multiple_of(first, rows), rows), :]
                packed[k][j][p] = jnp.where(row + first < count, block, jnp.zeros_like(block))
            return carry

        lax.fori_loop(0, room, one, 0)


def product_kernel(groups, room, blocks, rows, *refs):
    metas = refs[:groups]
    basis = refs[groups : 2 * groups]
    mine = refs[2 * groups : 3 * groups]
    other = refs[3 * groups : 4 * groups]
    keep, send, acc = refs[4 * groups :]
    core = lax.axis_index("mp")
    width = mine[0].shape[1]
    own_cols = pl.ds(pl.multiple_of(core * width, width), width)
    other_cols = pl.ds(pl.multiple_of((1 - core) * width, width), width)
    acc[...] = jnp.zeros_like(acc)
    for k in range(groups):

        def some(step, carry):
            sums = []
            for u in range(UNROLL):
                p = step * UNROLL + u
                label = metas[k][p]
                s = label % blocks
                at = pl.ds(pl.multiple_of(s * BLK, BLK), BLK)
                left = basis[k][p]
                a = jnp.dot(left, mine[k][at, :], preferred_element_type=jnp.float32)
                b = jnp.dot(left, other[k][at, :], preferred_element_type=jnp.float32)
                sums.append((label // blocks, a, b))
            for at, a, b in sums:
                acc[at, :, own_cols] += a
                acc[at, :, other_cols] += b
            return carry

        lax.fori_loop(0, room // UNROLL, some, 0)
    half = keep.shape[0]
    for o in range(half):
        keep[o] = acc[o * blocks : (o + 1) * blocks].astype(keep.dtype)
        send[o] = acc[(half + o) * blocks : (half + o + 1) * blocks].astype(send.dtype)


def combine_kernel(chunk, rows, border, count, *refs):
    mine, other = refs[:2]
    addends = refs[2 : 2 + count]
    combined, low, high = refs[2 + count :]
    blocks = combined.shape[0]
    core = lax.axis_index("mp")
    width = mine.shape[1]
    own_cols = pl.ds(pl.multiple_of(core * width, width), width)
    other_cols = pl.ds(pl.multiple_of((1 - core) * width, width), width)
    first = core * (rows * CHUNKS) + chunk * rows
    for b in range(blocks):
        at = pl.ds(pl.multiple_of(b * BLK + first, rows), rows)
        for cols, held in ((own_cols, mine), (other_cols, other)):
            total = held[at, :].astype(jnp.float32)
            for part in addends:
                total = total + part[0, b, :, cols].astype(jnp.float32)
            combined[b, :, cols] = total.astype(combined.dtype)
    low[...] = combined[:border]
    high[...] = combined[border : 2 * border]


def mlp_kernel(chunk, rows, border, reverse, valid, combined, before, after, *refs):
    in_own, in_other, out_own, out_other, final_own, final_other, state = refs
    blocks, _, width = combined.shape
    core = lax.axis_index("mp")
    first = core * (rows * CHUNKS) + chunk * rows
    for b in range(blocks):
        within = reverse[b] % blocks
        if b < border:
            pair = before[jnp.clip(within - border, 0, border - 1)]
        elif b < 2 * border:
            pair = after[jnp.clip(within, 0, border - 1)]
        else:
            pair = combined[within]
        state[b * rows : (b + 1) * rows] = (
            combined[b].astype(jnp.float32) + pair.astype(jnp.float32)
        ) * pair_scale
    for layer in range(MLPS):
        layer_input = state[...].astype(jnp.bfloat16)
        total = state[...]
        for w_in, w_out in ((in_own, out_own), (in_other, out_other)):
            value = jnp.dot(layer_input, w_in[layer], preferred_element_type=jnp.float32)
            hidden = (value / (1.0 + jnp.exp(-value))).astype(jnp.bfloat16)
            total = total + jnp.dot(hidden, w_out[layer], preferred_element_type=jnp.float32)
        state[...] = total
    half = width // 2
    own_cols = pl.ds(pl.multiple_of(core * half, half), half)
    other_cols = pl.ds(pl.multiple_of((1 - core) * half, half), half)
    row = lax.broadcasted_iota(jnp.int32, (rows, half), 0) + first
    limit = valid[0]
    for b in range(blocks):
        keep = row + b * BLK < limit
        at = slice(b * rows, (b + 1) * rows)
        final_own[b] = jnp.where(keep, state[at, own_cols], 0.0).astype(final_own.dtype)
        final_other[b] = jnp.where(keep, state[at, other_cols], 0.0).astype(final_other.dtype)


def join_kernel(rows, *refs):
    own, came, out = refs[:CHUNKS], refs[CHUNKS : 2 * CHUNKS], refs[2 * CHUNKS]
    blocks = own[0].shape[0]
    core = lax.axis_index("mp")
    for b in range(blocks):
        for j in range(CHUNKS):
            here = b * BLK + core * (rows * CHUNKS) + j * rows
            there = b * BLK + (1 - core) * (rows * CHUNKS) + j * rows
            out[pl.ds(pl.multiple_of(here, rows), rows), :] = own[j][b]
            out[pl.ds(pl.multiple_of(there, rows), rows), :] = came[j][b]


def local(
    messages,
    basis_blocks,
    source_block,
    target_owner,
    target_block,
    row_counts,
    reverse_block,
    valid_edges,
    weight_in,
    weight_out,
):
    devices = lax.axis_size("graph")
    edge_rows, part_width = messages.shape
    width = part_width * lax.axis_size("mp")
    blocks = edge_rows // BLK
    slots = source_block.shape[0]
    capacity = max(2, (slots + devices - 1) // devices + 1)
    border = blocks // 4
    near, far = split_bits(devices)
    groups = 1 << len(near)
    owners = devices // groups
    room = min(slots, capacity * owners)
    room = -(-room // UNROLL) * UNROLL
    rows = BLK // lax.axis_size("mp") // CHUNKS
    params = pltpu.CompilerParams(vmem_limit_bytes=VMEM_LIMIT)
    bf16 = jnp.bfloat16

    def near_send(array, k):
        return lax.ppermute(array, "graph", xor_pairs(devices, near_mask(near, k)))

    def swap(array):
        return lax.ppermute(array, "mp", [(0, 1), (1, 0)])

    mine = [messages] + [near_send(messages, k) for k in range(1, groups)]

    packed_shape = jax.ShapeDtypeStruct((room, rows, BLK), bf16)
    meta_shape = jax.ShapeDtypeStruct((room,), jnp.int32)
    packed = pl.pallas_call(
        functools.partial(pack_kernel, near, far, room, rows, blocks),
        out_shape=[packed_shape] * (groups * CHUNKS) + [meta_shape] * groups,
        in_specs=[smem()] * 4 + [full(None)],
        out_specs=[full(None)] * (groups * CHUNKS) + [smem()] * groups,
        scratch_shapes=[pltpu.SMEM((groups * room,), jnp.int32), pltpu.SMEM((groups,), jnp.int32)],
        compiler_params=params,
        name="pack",
    )(target_owner[:, 0], source_block, target_block, row_counts, basis_blocks)
    sent_basis = [packed[k * CHUNKS : (k + 1) * CHUNKS] for k in range(groups)]
    sent_meta = packed[groups * CHUNKS :]
    metas = [sent_meta[0]] + [near_send(sent_meta[k], k) for k in range(1, groups)]
    basis = [
        [sent_basis[0][j]] + [near_send(sent_basis[k][j], k) for k in range(1, groups)]
        for j in range(CHUNKS)
    ]
    other = [swap(array) for array in mine]
    in_other, out_other = swap(weight_in), swap(weight_out)

    half_shape = jax.ShapeDtypeStruct((owners // 2, blocks, rows, width), bf16)
    block_shape = jax.ShapeDtypeStruct((blocks, rows, width), bf16)
    border_shape = jax.ShapeDtypeStruct((border, rows, width), bf16)
    part_shape = jax.ShapeDtypeStruct((blocks, rows, part_width), bf16)
    up = [(i, (i + 1) % devices) for i in range(devices)]
    down = [(j, i) for i, j in up]
    finals = []
    for chunk in range(CHUNKS):
        keep, send = pl.pallas_call(
            functools.partial(product_kernel, groups, room, blocks, rows),
            out_shape=[half_shape] * 2,
            in_specs=[smem()] * groups + [full(None)] * (3 * groups),
            out_specs=[full(None)] * 2,
            scratch_shapes=[pltpu.VMEM((owners * blocks, rows, width), jnp.float32)],
            compiler_params=params,
            name="product",
        )(*metas, *basis[chunk], *mine, *other)
        addends = [keep]
        size = owners // 2
        for index, bit in enumerate(far):
            addends.append(lax.ppermute(send, "graph", xor_pairs(devices, 1 << bit)))
            if index + 1 < len(far):
                size = size // 2
                total = sum(part[size : 2 * size].astype(jnp.float32) for part in addends)
                send = total.astype(bf16)
        first_owner = pl.BlockSpec((1, blocks, rows, width), lambda i: (0, 0, 0, 0))

        def whole(*shape):
            return pl.BlockSpec(shape, lambda i: (0,) * len(shape))

        combined, low, high = pl.pallas_call(
            functools.partial(combine_kernel, chunk, rows, border, len(addends)),
            grid=(1,),
            out_shape=[block_shape, border_shape, border_shape],
            in_specs=[whole(edge_rows, part_width)] * 2 + [first_owner] * len(addends),
            out_specs=[whole(blocks, rows, width)] + [whole(border, rows, width)] * 2,
            compiler_params=params,
            name="combine",
        )(mine[0], other[0], *addends)
        before = lax.ppermute(high, "graph", up)
        after = lax.ppermute(low, "graph", down)
        own, theirs = pl.pallas_call(
            functools.partial(mlp_kernel, chunk, rows, border),
            out_shape=[part_shape] * 2,
            in_specs=[smem()] * 2 + [full(None)] * 7,
            out_specs=[full(None)] * 2,
            scratch_shapes=[pltpu.VMEM((blocks * rows, width), jnp.float32)],
            compiler_params=params,
            name="mlp",
        )(
            reverse_block,
            valid_edges,
            combined,
            before,
            after,
            weight_in,
            in_other,
            weight_out,
            out_other,
        )
        finals.append((own, swap(theirs)))

    return pl.pallas_call(
        functools.partial(join_kernel, rows),
        out_shape=jax.ShapeDtypeStruct(messages.shape, bf16),
        in_specs=[full(None)] * (2 * CHUNKS),
        out_specs=full(None),
        compiler_params=params,
        name="join",
    )(*[own for own, _ in finals], *[came for _, came in finals])


def solution(mesh):
    in_specs = (
        P("graph", "mp"),
        P("graph", None, None),
        P("graph"),
        P("graph", None),
        P("graph"),
        P("graph"),
        P("graph"),
        P("graph"),
        P(None, None, "mp"),
        P(None, "mp", None),
    )
    out_specs = P("graph", "mp")
    return jax.shard_map(local, mesh=mesh, in_specs=in_specs, out_specs=out_specs, check_vma=False)
```

```python
import functools

import jax
import jax.numpy as jnp
from jax import lax
from jax.experimental import pallas as pl
from jax.experimental.pallas import tpu as pltpu
from jax.sharding import PartitionSpec as P

MLPS = 3
BLK = 128
CHUNKS = 2
UNROLL = 14
GRANT = 12 * 1024 * 1024

pair_scale = 0.7071067811865476


def split_bits(devices):
    count = devices.bit_length() - 1
    near = [bit for bit in (0, 2) if bit < count]
    far = [bit for bit in range(count) if bit not in near]
    return near, far


def xor_pairs(devices, mask):
    return [(i, i ^ mask) for i in range(devices)]


def near_mask(near, k):
    return sum(((k >> i) & 1) << bit for i, bit in enumerate(near))


def grant(extra=0):
    return pltpu.CompilerParams(vmem_limit_bytes=GRANT + extra)


def spent(microseconds):
    return pl.CostEstimate(
        flops=0, bytes_accessed=int(microseconds * 3.69e6), transcendentals=0
    )


def after_all(value, *others):
    if not others:
        return value
    return lax.optimization_barrier((value, *others))[0]


def full(shape):
    return pl.BlockSpec(memory_space=pltpu.VMEM)


def smem():
    return pl.BlockSpec(memory_space=pltpu.SMEM)


def pack_kernel(near, far, room, rows, blocks, owner, source, target, counts, basis, *refs):
    groups = 1 << len(near)
    packed = refs[:groups]
    table, fill = refs[groups:]
    slots = basis.shape[0]
    me = lax.axis_index("graph")
    core = lax.axis_index("mp")
    for k in range(groups):
        fill[k] = 0

    def clear(i, carry):
        table[i] = -1
        return carry

    lax.fori_loop(0, groups * room, clear, 0, unroll=4)

    def route(t, carry):
        rel = owner[t] ^ me
        k = 0
        for i, bit in enumerate(near):
            k = k + (((rel >> bit) & 1) << i)
        p = fill[k]
        fill[k] = p + 1
        table[k * room + p] = t
        return carry

    lax.fori_loop(0, slots, route, 0)

    share = rows * CHUNKS
    first = core * share
    row = lax.broadcasted_iota(jnp.int32, (share, BLK), 0)
    label_row = lax.broadcasted_iota(jnp.int32, (rows, BLK), 0)
    lane = lax.broadcasted_iota(jnp.int32, (rows, BLK), 1)
    for k in range(groups):

        def one(p, labels):
            t = table[k * room + p]
            there = t >= 0
            s = jnp.maximum(t, 0)
            rel = owner[s] ^ me
            b = 0
            for i, bit in enumerate(far):
                b = b + (((rel >> bit) & 1) << (len(far) - 1 - i))
            place = jnp.where(there, b * blocks + target[s], 0)
            place = jnp.where(label_row == 0, place, source[s])
            labels = jnp.where(lane == p, place, labels)
            count = jnp.where(there, counts[s], 0)
            block = basis[s, pl.ds(pl.multiple_of(first, share), share), :]
            block = jnp.where(row + first < count, block, jnp.zeros_like(block))
            packed[k][p] = block
            return labels

        labels = lax.fori_loop(0, room, one, jnp.zeros((rows, BLK), jnp.int32), unroll=2)
        labels = labels.astype(jnp.float32).astype(jnp.bfloat16)
        packed[k][room, :rows] = labels


def add_products(room, held, basis, mine, other, acc, staged, metas, sem):
    sources = len(basis)
    core = lax.axis_index("mp")
    width = mine[0].shape[1]
    own_cols = pl.ds(pl.multiple_of(core * width, width), width)
    other_cols = pl.ds(pl.multiple_of((1 - core) * width, width), width)
    for k in range(sources):
        staged[k] = basis[k][room, :16, :].astype(jnp.float32).astype(jnp.int32)
    copy = pltpu.make_async_copy(staged, metas, sem)
    copy.start()
    acc[...] = jnp.zeros_like(acc)
    copy.wait()
    for k in range(sources):

        def some(step, carry):
            sums = []
            for u in range(UNROLL):
                p = step * UNROLL + u
                s = metas[k, 1, p]
                at = pl.ds(pl.multiple_of(s * BLK, BLK), BLK)
                left = basis[k][p, held]
                a = jnp.dot(left, mine[k][at, :], preferred_element_type=jnp.float32)
                b = jnp.dot(left, other[k][at, :], preferred_element_type=jnp.float32)
                sums.append((metas[k, 0, p], a, b))
            for at, a, b in sums:
                acc[at, :, own_cols] += a
                acc[at, :, other_cols] += b
            return carry

        lax.fori_loop(0, room // UNROLL, some, 0)


def first_kernel(sources, room, *refs):
    basis, mine, other = (refs[i * sources : (i + 1) * sources] for i in range(3))
    acc, staged, metas, sem = refs[3 * sources :]
    add_products(room, slice(None), basis, mine, other, acc, staged, metas, sem)


def last_kernel(sources, room, blocks, rows, chunk, *refs):
    basis, mine, other = (refs[i * sources : (i + 1) * sources] for i in range(3))
    before = refs[3 * sources]
    keep_low, keep_high, send_low, send_high, acc, staged, metas, sem = refs[3 * sources + 1 :]
    held = slice(chunk * rows, (chunk + 1) * rows)
    add_products(room, held, basis, mine, other, acc, staged, metas, sem)
    part = keep_low.shape[0]
    for i, out in enumerate((keep_low, keep_high, send_low, send_high)):
        for o in range(part):
            at = slice((i * part + o) * blocks, (i * part + o + 1) * blocks)
            out[o] = (before[at, held] + acc[at]).astype(out.dtype)


def combine_kernel(chunk, rows, border, count, *refs):
    mine, other = refs[:2]
    addends = refs[2 : 2 + count]
    combined, even_send, odd_send = refs[2 + count :]
    blocks = combined.shape[0]
    core = lax.axis_index("mp")
    width = mine.shape[1]
    own_cols = pl.ds(pl.multiple_of(core * width, width), width)
    other_cols = pl.ds(pl.multiple_of((1 - core) * width, width), width)
    first = core * (rows * CHUNKS) + chunk * rows
    for b in range(blocks):
        at = pl.ds(pl.multiple_of(b * BLK + first, rows), rows)
        for cols, held in ((own_cols, mine), (other_cols, other)):
            total = held[at, :].astype(jnp.float32)
            for part in addends:
                total = total + part[0, b, :, cols].astype(jnp.float32)
            combined[b, :, cols] = total.astype(combined.dtype)
    odd = lax.axis_index("graph") % 2
    even_send[...] = combined[pl.ds((1 - odd) * border, border)]
    odd_send[...] = combined[pl.ds(odd * border, border)]


def mlp_kernel(chunk, rows, border, reverse, valid, combined, even_came, odd_came, *refs):
    in_own, in_other, out_own, out_other, final_own, final_other, state = refs
    blocks, _, width = combined.shape
    core = lax.axis_index("mp")
    odd = lax.axis_index("graph") % 2 == 1
    first = core * (rows * CHUNKS) + chunk * rows
    for b in range(blocks):
        within = reverse[b] % blocks
        if b >= 2 * border:
            pair = combined[within]
        else:
            w = jnp.clip(within - (border if b < border else 0), 0, border - 1)
            pair = jnp.where(odd == (b < border), even_came[w], odd_came[w])
        state[b * rows : (b + 1) * rows] = (
            combined[b].astype(jnp.float32) + pair.astype(jnp.float32)
        ) * pair_scale
    for layer in range(MLPS):
        layer_input = state[...].astype(jnp.bfloat16)
        total = state[...]
        for w_in, w_out in ((in_own, out_own), (in_other, out_other)):
            value = jnp.dot(layer_input, w_in[layer], preferred_element_type=jnp.float32)
            hidden = (value / (1.0 + jnp.exp(-value))).astype(jnp.bfloat16)
            total = total + jnp.dot(hidden, w_out[layer], preferred_element_type=jnp.float32)
        state[...] = total
    half = width // 2
    own_cols = pl.ds(pl.multiple_of(core * half, half), half)
    other_cols = pl.ds(pl.multiple_of((1 - core) * half, half), half)
    row = lax.broadcasted_iota(jnp.int32, (rows, half), 0) + first
    limit = valid[0]
    for b in range(blocks):
        keep = row + b * BLK < limit
        at = slice(b * rows, (b + 1) * rows)
        final_own[b] = jnp.where(keep, state[at, own_cols], 0.0).astype(final_own.dtype)
        final_other[b] = jnp.where(keep, state[at, other_cols], 0.0).astype(final_other.dtype)


def join_kernel(rows, *refs):
    own, came, out = refs[:CHUNKS], refs[CHUNKS : 2 * CHUNKS], refs[2 * CHUNKS]
    core = lax.axis_index("mp")
    for chunk in range(CHUNKS):
        for b in range(own[chunk].shape[0]):
            base = b * BLK + chunk * rows
            here = base + core * (rows * CHUNKS)
            there = base + (1 - core) * (rows * CHUNKS)
            out[pl.ds(pl.multiple_of(here, rows), rows), :] = own[chunk][b]
            out[pl.ds(pl.multiple_of(there, rows), rows), :] = came[chunk][b]


def local(
    messages,
    basis_blocks,
    source_block,
    target_owner,
    target_block,
    row_counts,
    reverse_block,
    valid_edges,
    weight_in,
    weight_out,
):
    devices = lax.axis_size("graph")
    edge_rows, part_width = messages.shape
    width = part_width * lax.axis_size("mp")
    blocks = edge_rows // BLK
    slots = source_block.shape[0]
    capacity = max(2, (slots + devices - 1) // devices + 1)
    border = blocks // 4
    near, far = split_bits(devices)
    groups = 1 << len(near)
    owners = devices // groups
    room = min(slots, capacity * owners)
    room = -(-room // UNROLL) * UNROLL
    rows = BLK // lax.axis_size("mp") // CHUNKS
    bf16 = jnp.bfloat16

    def near_send(array, k):
        return lax.ppermute(array, "graph", xor_pairs(devices, near_mask(near, k)))

    def far_send(array, bit):
        return lax.ppermute(array, "graph", xor_pairs(devices, 1 << bit))

    def swap(array):
        return lax.ppermute(array, "mp", [(0, 1), (1, 0)])

    def swap_halves(array):
        middle = array.shape[0] // 2
        return jnp.concatenate([swap(array[:middle]), swap(array[middle:])], axis=0)

    mine = [messages, near_send(messages, 1), near_send(messages, 2)]
    other = [swap(messages)]
    in_other, out_other = swap(weight_in), swap(weight_out)

    share = rows * CHUNKS
    whole_shape = jax.ShapeDtypeStruct((room + 1, share, BLK), bf16)
    packed = pl.pallas_call(
        functools.partial(pack_kernel, near, far, room, rows, blocks),
        out_shape=[whole_shape] * groups,
        in_specs=[smem()] * 4 + [full(None)],
        out_specs=[full(None)] * groups,
        scratch_shapes=[pltpu.SMEM((groups * room,), jnp.int32), pltpu.SMEM((groups,), jnp.int32)],
        compiler_params=grant(),
        cost_estimate=spent(6),
        name="pack",
    )(
        target_owner[:, 0],
        source_block,
        target_block,
        row_counts,
        after_all(basis_blocks, other[0], in_other, out_other),
    )
    last = groups - 1
    middle = edge_rows // 2
    acc_shape = (owners * blocks, rows, width)
    acc_bytes = owners * blocks * rows * width * 4
    partial = pl.pallas_call(
        functools.partial(first_kernel, 1, room),
        out_shape=jax.ShapeDtypeStruct((owners * blocks, share, width), jnp.float32),
        in_specs=[full(None)] * 3,
        out_specs=full(None),
        scratch_shapes=[
            pltpu.VMEM((1, 16, BLK), jnp.int32),
            pltpu.SMEM((1, 16, BLK), jnp.int32),
            pltpu.SemaphoreType.DMA,
        ],
        compiler_params=grant(CHUNKS * acc_bytes),
        cost_estimate=spent(2),
        name="own_products",
    )(packed[0], messages, other[0])

    basis = [packed[0]]
    for k in range(1, groups):
        basis.append(near_send(after_all(packed[k], partial), k))
    mine = [messages] + [after_all(array, partial) for array in mine[1:]]
    onward = [near_send(mine[1][:middle], 2), near_send(mine[2][middle:], 1)]
    mine.append(jnp.concatenate(onward, axis=0))
    other.extend(swap_halves(mine[k]) for k in range(1, groups))

    part_owners_shape = jax.ShapeDtypeStruct((owners // 4, blocks, rows, width), bf16)
    block_shape = jax.ShapeDtypeStruct((blocks, rows, width), bf16)
    part_shape = jax.ShapeDtypeStruct((blocks, rows, part_width), bf16)
    border_shape = jax.ShapeDtypeStruct((border, rows, width), bf16)
    even_pairs = [(i, i ^ 1) for i in range(devices)]
    odd_pairs = [(i, (i + 1 if i % 2 else i - 1) % devices) for i in range(devices)]
    summed = []
    for chunk in range(CHUNKS):
        summed.append(
            pl.pallas_call(
                functools.partial(last_kernel, last, room, blocks, rows, chunk),
                out_shape=[part_owners_shape] * 4,
                in_specs=[full(None)] * (3 * last + 1),
                out_specs=[full(None)] * 4,
                scratch_shapes=[
                    pltpu.VMEM(acc_shape, jnp.float32),
                    pltpu.VMEM((last, 16, BLK), jnp.int32),
                    pltpu.SMEM((last, 16, BLK), jnp.int32),
                    pltpu.SemaphoreType.DMA,
                ],
                compiler_params=grant(4 * acc_bytes),
                cost_estimate=spent(2),
                name="came_products",
            )(*basis[1:], *mine[1:], *other[1:], partial)
        )
    came_high = [far_send(parts[3], far[0]) for parts in summed]
    came_low = [far_send(after_all(parts[2], came_high[-1]), far[0]) for parts in summed]
    finals = []
    for chunk in range(CHUNKS):
        keep_low, keep_high = summed[chunk][:2]
        send = (keep_high.astype(jnp.float32) + came_high[chunk].astype(jnp.float32)).astype(bf16)
        addends = [keep_low, came_low[chunk]]
        size = owners // 4
        for index, bit in enumerate(far[1:]):
            addends.append(far_send(send, bit))
            if index + 2 < len(far):
                size = size // 2
                total = sum(part[size : 2 * size].astype(jnp.float32) for part in addends)
                send = total.astype(bf16)
        combined, even_send, odd_send = pl.pallas_call(
            functools.partial(combine_kernel, chunk, rows, border, len(addends)),
            out_shape=[block_shape, border_shape, border_shape],
            in_specs=[full(None)] * (2 + len(addends)),
            out_specs=[full(None)] * 3,
            compiler_params=grant(acc_bytes),
            cost_estimate=spent(0.5),
            name="combine",
        )(mine[0], other[0], *addends)
        came = [
            lax.ppermute(even_send, "graph", even_pairs),
            lax.ppermute(odd_send, "graph", odd_pairs),
        ]
        own, theirs = pl.pallas_call(
            functools.partial(mlp_kernel, chunk, rows, border),
            out_shape=[part_shape] * 2,
            in_specs=[smem()] * 2 + [full(None)] * 7,
            out_specs=[full(None)] * 2,
            scratch_shapes=[pltpu.VMEM((blocks * rows, width), jnp.float32)],
            compiler_params=grant(),
            cost_estimate=spent(2),
            name="mlp",
        )(
            reverse_block,
            valid_edges,
            combined,
            *came,
            weight_in,
            in_other,
            weight_out,
            out_other,
        )
        finals.append((own, swap(theirs)))

    return pl.pallas_call(
        functools.partial(join_kernel, rows),
        out_shape=jax.ShapeDtypeStruct(messages.shape, bf16),
        in_specs=[full(None)] * (2 * CHUNKS),
        out_specs=full(None),
        compiler_params=grant(),
        cost_estimate=spent(1),
        name="join",
    )(*[own for own, _ in finals], *[came for _, came in finals])


def solution(mesh):
    in_specs = (
        P("graph", "mp"),
        P("graph", None, None),
        P("graph"),
        P("graph", None),
        P("graph"),
        P("graph"),
        P("graph"),
        P("graph"),
        P(None, None, "mp"),
        P(None, "mp", None),
    )
    out_specs = P("graph", "mp")
    return jax.shard_map(local, mesh=mesh, in_specs=in_specs, out_specs=out_specs, check_vma=False)
```

```python
import functools

import jax
import jax.numpy as jnp
from jax import lax
from jax.experimental import pallas as pl
from jax.experimental.pallas import tpu as pltpu
from jax.sharding import PartitionSpec as P

MLPS = 3
BLK = 128
CHUNKS = 2
UNROLL = 14
GRANT = 12 * 1024 * 1024

pair_scale = 0.7071067811865476


def split_bits(devices):
    count = devices.bit_length() - 1
    near = [bit for bit in (0, 2) if bit < count]
    far = [bit for bit in range(count) if bit not in near]
    return near, far


def xor_pairs(devices, mask):
    return [(i, i ^ mask) for i in range(devices)]


def near_mask(near, k):
    return sum(((k >> i) & 1) << bit for i, bit in enumerate(near))


def grant(extra=0):
    return pltpu.CompilerParams(vmem_limit_bytes=GRANT + extra)


def spent(microseconds):
    return pl.CostEstimate(
        flops=0, bytes_accessed=int(microseconds * 3.69e6), transcendentals=0
    )


def after_all(value, *others):
    if not others:
        return value
    return lax.optimization_barrier((value, *others))[0]


def full(shape):
    return pl.BlockSpec(memory_space=pltpu.VMEM)


def smem():
    return pl.BlockSpec(memory_space=pltpu.SMEM)


def pack_kernel(near, far, room, rows, blocks, owner, source, target, counts, basis, *refs):
    groups = 1 << len(near)
    whole, cut = refs[: groups - 1], refs[groups - 1 : groups - 1 + CHUNKS]
    table, fill = refs[groups - 1 + CHUNKS :]
    slots = basis.shape[0]
    me = lax.axis_index("graph")
    core = lax.axis_index("mp")
    for k in range(groups):
        fill[k] = 0

    def clear(i, carry):
        table[i] = -1
        return carry

    lax.fori_loop(0, groups * room, clear, 0, unroll=4)

    def route(t, carry):
        rel = owner[t] ^ me
        k = 0
        for i, bit in enumerate(near):
            k = k + (((rel >> bit) & 1) << i)
        p = fill[k]
        fill[k] = p + 1
        table[k * room + p] = t
        return carry

    lax.fori_loop(0, slots, route, 0)

    share = rows * CHUNKS
    first = core * share
    row = lax.broadcasted_iota(jnp.int32, (share, BLK), 0)
    label_row = lax.broadcasted_iota(jnp.int32, (rows, BLK), 0)
    lane = lax.broadcasted_iota(jnp.int32, (rows, BLK), 1)
    for k in range(groups):

        def one(p, labels):
            t = table[k * room + p]
            there = t >= 0
            s = jnp.maximum(t, 0)
            rel = owner[s] ^ me
            b = 0
            for i, bit in enumerate(far):
                b = b + (((rel >> bit) & 1) << (len(far) - 1 - i))
            place = jnp.where(there, b * blocks + target[s], 0)
            place = jnp.where(label_row == 0, place, source[s])
            labels = jnp.where(lane == p, place, labels)
            count = jnp.where(there, counts[s], 0)
            block = basis[s, pl.ds(pl.multiple_of(first, share), share), :]
            block = jnp.where(row + first < count, block, jnp.zeros_like(block))
            if k < groups - 1:
                whole[k][p] = block
            else:
                for j in range(CHUNKS):
                    cut[j][p] = block[j * rows : (j + 1) * rows]
            return labels

        labels = lax.fori_loop(0, room, one, jnp.zeros((rows, BLK), jnp.int32), unroll=2)
        labels = labels.astype(jnp.float32).astype(jnp.bfloat16)
        if k < groups - 1:
            whole[k][room, :rows] = labels
        else:
            cut[0][room] = labels


def add_products(room, labels, basis, mine, other, acc, staged, metas, sem):
    sources = len(basis)
    core = lax.axis_index("mp")
    width = mine[0].shape[1]
    own_cols = pl.ds(pl.multiple_of(core * width, width), width)
    other_cols = pl.ds(pl.multiple_of((1 - core) * width, width), width)
    for k in range(sources):
        staged[k] = labels[k][room, :16, :].astype(jnp.float32).astype(jnp.int32)
    copy = pltpu.make_async_copy(staged, metas, sem)
    copy.start()
    acc[...] = jnp.zeros_like(acc)
    copy.wait()
    for k in range(sources):

        def some(step, carry):
            sums = []
            for u in range(UNROLL):
                p = step * UNROLL + u
                s = metas[k, 1, p]
                at = pl.ds(pl.multiple_of(s * BLK, BLK), BLK)
                left = basis[k][p]
                a = jnp.dot(left, mine[k][at, :], preferred_element_type=jnp.float32)
                b = jnp.dot(left, other[k][at, :], preferred_element_type=jnp.float32)
                sums.append((metas[k, 0, p], a, b))
            for at, a, b in sums:
                acc[at, :, own_cols] += a
                acc[at, :, other_cols] += b
            return carry

        lax.fori_loop(0, room // UNROLL, some, 0)


def first_kernel(sources, room, *refs):
    basis, mine, other = (refs[i * sources : (i + 1) * sources] for i in range(3))
    acc, staged, metas, sem = refs[3 * sources :]
    add_products(room, basis, basis, mine, other, acc, staged, metas, sem)


def last_kernel(room, blocks, rows, chunk, labels, basis, mine, other, before, *refs):
    keep_low, keep_high, send_low, send_high, acc, staged, metas, sem = refs
    held = slice(chunk * rows, (chunk + 1) * rows)
    add_products(room, [labels], [basis], [mine], [other], acc, staged, metas, sem)
    part = keep_low.shape[0]
    for i, out in enumerate((keep_low, keep_high, send_low, send_high)):
        for o in range(part):
            at = slice((i * part + o) * blocks, (i * part + o + 1) * blocks)
            out[o] = (before[at, held] + acc[at]).astype(out.dtype)


def combine_kernel(rows, border, start, bases, *refs):
    mine, other = refs[:2]
    counts = [len(each) for each in bases]
    addends, outs = refs[2 : 2 + sum(counts)], refs[2 + sum(counts) :]
    combined, sends = outs[0], outs[1:]
    core = lax.axis_index("mp")
    width = mine.shape[1]
    own_cols = pl.ds(pl.multiple_of(core * width, width), width)
    other_cols = pl.ds(pl.multiple_of((1 - core) * width, width), width)
    for chunk in range(CHUNKS):
        parts = addends[sum(counts[:chunk]) : sum(counts[: chunk + 1])]
        first = core * (rows * CHUNKS) + chunk * rows
        held_rows = slice(chunk * rows, (chunk + 1) * rows)
        for i in range(combined.shape[0]):
            b = start + i
            at = pl.ds(pl.multiple_of(b * BLK + first, rows), rows)
            for cols, held in ((own_cols, mine), (other_cols, other)):
                total = held[at, :].astype(jnp.float32)
                for part, base in zip(parts, bases[chunk]):
                    total = total + part[0, b - base, :, cols].astype(jnp.float32)
                combined[i, held_rows, cols] = total.astype(combined.dtype)
    if sends:
        odd = lax.axis_index("graph") % 2
        even_send, odd_send = sends
        even_send[...] = combined[pl.ds((1 - odd) * border, border)]
        odd_send[...] = combined[pl.ds(odd * border, border)]


def mlp_kernel(border, start, blocks, reverse, valid, combined, *refs):
    came, refs = (refs[:2], refs[2:]) if start == 0 else (None, refs)
    in_own, in_other, out_own, out_other, final_own, final_other, state = refs
    count, share, width = combined.shape
    core = lax.axis_index("mp")
    odd = lax.axis_index("graph") % 2 == 1
    first = core * share
    for i in range(count):
        b = start + i
        within = reverse[b] % blocks
        if came is None:
            pair = combined[within - start]
        else:
            w = jnp.clip(within - (border if b < border else 0), 0, border - 1)
            pair = jnp.where(odd == (b < border), came[0][w], came[1][w])
        state[i * share : (i + 1) * share] = (
            combined[i].astype(jnp.float32) + pair.astype(jnp.float32)
        ) * pair_scale
    for layer in range(MLPS):
        layer_input = state[...].astype(jnp.bfloat16)
        total = state[...]
        for w_in, w_out in ((in_own, out_own), (in_other, out_other)):
            value = jnp.dot(layer_input, w_in[layer], preferred_element_type=jnp.float32)
            hidden = (value / (1.0 + jnp.exp(-value))).astype(jnp.bfloat16)
            total = total + jnp.dot(hidden, w_out[layer], preferred_element_type=jnp.float32)
        state[...] = total
    half = width // 2
    own_cols = pl.ds(pl.multiple_of(core * half, half), half)
    other_cols = pl.ds(pl.multiple_of((1 - core) * half, half), half)
    row = lax.broadcasted_iota(jnp.int32, (share, half), 0) + first
    limit = valid[0]
    for i in range(count):
        keep = row + (start + i) * BLK < limit
        at = slice(i * share, (i + 1) * share)
        final_own[i] = jnp.where(keep, state[at, own_cols], 0.0).astype(final_own.dtype)
        final_other[i] = jnp.where(keep, state[at, other_cols], 0.0).astype(final_other.dtype)


def join_kernel(starts, *refs):
    parts = len(starts)
    own, came, out = refs[:parts], refs[parts : 2 * parts], refs[2 * parts]
    core = lax.axis_index("mp")
    for i, start in enumerate(starts):
        count, share, _ = own[i].shape
        for b in range(count):
            here = (start + b) * BLK + core * share
            there = (start + b) * BLK + (1 - core) * share
            out[pl.ds(pl.multiple_of(here, share), share), :] = own[i][b]
            out[pl.ds(pl.multiple_of(there, share), share), :] = came[i][b]


def local(
    messages,
    basis_blocks,
    source_block,
    target_owner,
    target_block,
    row_counts,
    reverse_block,
    valid_edges,
    weight_in,
    weight_out,
):
    devices = lax.axis_size("graph")
    edge_rows, part_width = messages.shape
    width = part_width * lax.axis_size("mp")
    blocks = edge_rows // BLK
    slots = source_block.shape[0]
    capacity = max(2, (slots + devices - 1) // devices + 1)
    border = blocks // 4
    near, far = split_bits(devices)
    groups = 1 << len(near)
    owners = devices // groups
    room = min(slots, capacity * owners)
    room = -(-room // UNROLL) * UNROLL
    rows = BLK // lax.axis_size("mp") // CHUNKS
    bf16 = jnp.bfloat16

    def near_send(array, k):
        return lax.ppermute(array, "graph", xor_pairs(devices, near_mask(near, k)))

    def far_send(array, bit):
        return lax.ppermute(array, "graph", xor_pairs(devices, 1 << bit))

    def swap(array):
        return lax.ppermute(array, "mp", [(0, 1), (1, 0)])

    mine = [messages, near_send(messages, 1), near_send(messages, 2)]
    other = [swap(messages)]
    in_other, out_other = swap(weight_in), swap(weight_out)

    share = rows * CHUNKS
    whole_shape = jax.ShapeDtypeStruct((room + 1, share, BLK), bf16)
    cut_shapes = [
        jax.ShapeDtypeStruct((room + (j == 0), rows, BLK), bf16) for j in range(CHUNKS)
    ]
    packed = pl.pallas_call(
        functools.partial(pack_kernel, near, far, room, rows, blocks),
        out_shape=[whole_shape] * (groups - 1) + cut_shapes,
        in_specs=[smem()] * 4 + [full(None)],
        out_specs=[full(None)] * (groups - 1 + CHUNKS),
        scratch_shapes=[pltpu.SMEM((groups * room,), jnp.int32), pltpu.SMEM((groups,), jnp.int32)],
        compiler_params=grant(),
        cost_estimate=spent(6),
        name="pack",
    )(
        target_owner[:, 0],
        source_block,
        target_block,
        row_counts,
        after_all(basis_blocks, other[0], in_other, out_other),
    )
    last = groups - 1
    middle = edge_rows // 2
    basis = [packed[0]]
    for k in range(1, last):
        basis.append(near_send(after_all(packed[k], *mine[1:]), k))
    ready = [after_all(array, packed[0]) for array in mine[1:]]
    onward = [near_send(ready[0][:middle], 2), near_send(ready[1][middle:], 1)]
    mine.append(jnp.concatenate(onward, axis=0))
    other.extend(swap(after_all(array, *basis[1:])) for array in mine[1:])
    acc_shape = (owners * blocks, rows, width)
    acc_bytes = owners * blocks * rows * width * 4
    partial = pl.pallas_call(
        functools.partial(first_kernel, last, room),
        out_shape=jax.ShapeDtypeStruct((owners * blocks, share, width), jnp.float32),
        in_specs=[full(None)] * (3 * last),
        out_specs=full(None),
        scratch_shapes=[
            pltpu.VMEM((last, 16, BLK), jnp.int32),
            pltpu.SMEM((last, 16, BLK), jnp.int32),
            pltpu.SemaphoreType.DMA,
        ],
        compiler_params=grant(CHUNKS * acc_bytes),
        cost_estimate=spent(4),
        name="first_products",
    )(*basis[:last], *mine[:last], *other[:last])

    part_owners_shape = jax.ShapeDtypeStruct((owners // 4, blocks, rows, width), bf16)
    border_shape = jax.ShapeDtypeStruct((border, share, width), bf16)
    even_pairs = [(i, i ^ 1) for i in range(devices)]
    odd_pairs = [(i, (i + 1 if i % 2 else i - 1) % devices) for i in range(devices)]
    cut, waited, came_first = [], basis[1:], None
    sums, lows, highs = [], [], []
    for chunk in range(CHUNKS):
        cut.append(near_send(after_all(packed[last + chunk], *waited), last))
        waits = [] if came_first is None else [came_first]
        keep_low, keep_high, send_low, send_high = pl.pallas_call(
            functools.partial(last_kernel, room, blocks, rows, chunk),
            out_shape=[part_owners_shape] * 4,
            in_specs=[full(None)] * 5,
            out_specs=[full(None)] * 4,
            scratch_shapes=[
                pltpu.VMEM(acc_shape, jnp.float32),
                pltpu.VMEM((1, 16, BLK), jnp.int32),
                pltpu.SMEM((1, 16, BLK), jnp.int32),
                pltpu.SemaphoreType.DMA,
            ],
            compiler_params=grant(4 * acc_bytes),
            cost_estimate=spent(2),
            name="last_products",
        )(cut[0], after_all(cut[chunk], *waits), mine[last], other[last], partial)
        waited = [keep_low]
        came = far_send(send_high, far[0])
        came_first = (keep_high.astype(jnp.float32) + came.astype(jnp.float32)).astype(bf16)
        sums.append(came_first)
        highs.append(came)
        lows.append((keep_low, send_low))
    lows = [
        (keep_low, far_send(after_all(send_low, came), far[0]))
        for (keep_low, send_low), came in zip(lows, highs)
    ]
    starts = [0, 2 * border]
    stops = [2 * border, blocks]
    arrived = []
    for chunk in range(CHUNKS):
        pieces = [(0, blocks)] if chunk < CHUNKS - 1 else list(zip(starts, stops))
        found = []
        for start, stop in pieces:
            send, addends, bases = sums[chunk][:, start:stop], list(lows[chunk]), [0, 0]
            size = owners // 4
            for index, bit in enumerate(far[1:]):
                addends.append(far_send(send, bit))
                bases.append(start)
                if index + 2 < len(far):
                    size = size // 2
                    send = sum(
                        part[size : 2 * size, start - base : stop - base].astype(jnp.float32)
                        for part, base in zip(addends, bases)
                    ).astype(bf16)
            found.append((addends, tuple(bases)))
        arrived.append(found if len(found) > 1 else found * 2)
    finals, came = [], []
    for index, (start, stop) in enumerate(zip(starts, stops)):
        addends = [array for found in arrived for array in found[index][0]]
        bases = tuple(found[index][1] for found in arrived)
        piece_shape = jax.ShapeDtypeStruct((stop - start, share, width), bf16)
        part_shape = jax.ShapeDtypeStruct((stop - start, share, part_width), bf16)
        outs = pl.pallas_call(
            functools.partial(combine_kernel, rows, border, start, bases),
            out_shape=[piece_shape] + [border_shape] * (2 if start == 0 else 0),
            in_specs=[full(None)] * (2 + len(addends)),
            out_specs=[full(None)] * (3 if start == 0 else 1),
            compiler_params=grant(acc_bytes),
            cost_estimate=spent(0.5),
            name="combine",
        )(mine[0], other[0], *addends)
        if start == 0:
            came = [
                lax.ppermute(outs[2], "graph", odd_pairs),
                lax.ppermute(outs[1], "graph", even_pairs),
            ][::-1]
        operands = [outs[0]] + (came if start == 0 else [])
        own, theirs = pl.pallas_call(
            functools.partial(mlp_kernel, border, start, blocks),
            out_shape=[part_shape] * 2,
            in_specs=[smem()] * 2 + [full(None)] * (4 + len(operands)),
            out_specs=[full(None)] * 2,
            scratch_shapes=[pltpu.VMEM(((stop - start) * share, width), jnp.float32)],
            compiler_params=grant(),
            cost_estimate=spent(2),
            name="mlp",
        )(reverse_block, valid_edges, *operands, weight_in, in_other, weight_out, out_other)
        finals.append((own, swap(theirs)))

    return pl.pallas_call(
        functools.partial(join_kernel, starts),
        out_shape=jax.ShapeDtypeStruct(messages.shape, bf16),
        in_specs=[full(None)] * (2 * len(finals)),
        out_specs=full(None),
        compiler_params=grant(),
        cost_estimate=spent(1),
        name="join",
    )(*[own for own, _ in finals], *[theirs for _, theirs in finals])


def solution(mesh):
    in_specs = (
        P("graph", "mp"),
        P("graph", None, None),
        P("graph"),
        P("graph", None),
        P("graph"),
        P("graph"),
        P("graph"),
        P("graph"),
        P(None, None, "mp"),
        P(None, "mp", None),
    )
    out_specs = P("graph", "mp")
    return jax.shard_map(local, mesh=mesh, in_specs=in_specs, out_specs=out_specs, check_vma=False)
```

```python
import functools

import jax
import jax.numpy as jnp
from jax import lax
from jax.experimental import pallas as pl
from jax.experimental.pallas import tpu as pltpu
from jax.sharding import PartitionSpec as P

MLPS = 3
BLK = 128
CHUNKS = 2
UNROLL = 14
GRANT = 12 * 1024 * 1024

pair_scale = 0.7071067811865476


def split_bits(devices):
    count = devices.bit_length() - 1
    near = [bit for bit in (0, 2) if bit < count]
    far = [bit for bit in range(count) if bit not in near]
    return near, far


def xor_pairs(devices, mask):
    return [(i, i ^ mask) for i in range(devices)]


def near_mask(near, k):
    return sum(((k >> i) & 1) << bit for i, bit in enumerate(near))


def grant(extra=0):
    return pltpu.CompilerParams(vmem_limit_bytes=GRANT + extra)


def spent(microseconds):
    return pl.CostEstimate(
        flops=0, bytes_accessed=int(microseconds * 3.69e6), transcendentals=0
    )


def after_all(value, *others):
    if not others:
        return value
    return lax.optimization_barrier((value, *others))[0]


def full(shape):
    return pl.BlockSpec(memory_space=pltpu.VMEM)


def smem():
    return pl.BlockSpec(memory_space=pltpu.SMEM)


def pack_kernel(near, far, room, rows, blocks, owner, source, target, counts, basis, *refs):
    groups = 1 << len(near)
    whole, cut = refs[: groups - 1], refs[groups - 1 : groups - 1 + CHUNKS]
    table, fill = refs[groups - 1 + CHUNKS :]
    slots = basis.shape[0]
    me = lax.axis_index("graph")
    core = lax.axis_index("mp")
    for k in range(groups):
        fill[k] = 0

    def clear(i, carry):
        table[i] = -1
        return carry

    lax.fori_loop(0, groups * room, clear, 0, unroll=4)

    def route(t, carry):
        rel = owner[t] ^ me
        k = 0
        for i, bit in enumerate(near):
            k = k + (((rel >> bit) & 1) << i)
        p = fill[k]
        fill[k] = p + 1
        table[k * room + p] = t
        return carry

    lax.fori_loop(0, slots, route, 0)

    share = rows * CHUNKS
    first = core * share
    row = lax.broadcasted_iota(jnp.int32, (share, BLK), 0)
    label_row = lax.broadcasted_iota(jnp.int32, (rows, BLK), 0)
    lane = lax.broadcasted_iota(jnp.int32, (rows, BLK), 1)
    for k in range(groups):

        def one(p, labels):
            t = table[k * room + p]
            there = t >= 0
            s = jnp.maximum(t, 0)
            rel = owner[s] ^ me
            b = 0
            for i, bit in enumerate(far):
                b = b + (((rel >> bit) & 1) << (len(far) - 1 - i))
            place = jnp.where(there, b * blocks + target[s], 0)
            place = jnp.where(label_row == 0, place, source[s])
            labels = jnp.where(lane == p, place, labels)
            count = jnp.where(there, counts[s], 0)
            block = basis[s, pl.ds(pl.multiple_of(first, share), share), :]
            block = jnp.where(row + first < count, block, jnp.zeros_like(block))
            if k < groups - 1:
                whole[k][p] = block
            else:
                for j in range(CHUNKS):
                    cut[j][p] = block[j * rows : (j + 1) * rows]
            return labels

        labels = lax.fori_loop(0, room, one, jnp.zeros((rows, BLK), jnp.int32), unroll=2)
        labels = labels.astype(jnp.float32).astype(jnp.bfloat16)
        if k < groups - 1:
            whole[k][room, :rows] = labels
        else:
            cut[0][room] = labels


def add_products(room, labels, basis, mine, other, acc, staged, metas, sem):
    sources = len(basis)
    core = lax.axis_index("mp")
    width = mine[0].shape[1]
    own_cols = pl.ds(pl.multiple_of(core * width, width), width)
    other_cols = pl.ds(pl.multiple_of((1 - core) * width, width), width)
    for k in range(sources):
        staged[k] = labels[k][room, :16, :].astype(jnp.float32).astype(jnp.int32)
    copy = pltpu.make_async_copy(staged, metas, sem)
    copy.start()
    acc[...] = jnp.zeros_like(acc)
    copy.wait()
    for k in range(sources):

        def some(step, carry):
            sums = []
            for u in range(UNROLL):
                p = step * UNROLL + u
                s = metas[k, 1, p]
                at = pl.ds(pl.multiple_of(s * BLK, BLK), BLK)
                left = basis[k][p]
                a = jnp.dot(left, mine[k][at, :], preferred_element_type=jnp.float32)
                b = jnp.dot(left, other[k][at, :], preferred_element_type=jnp.float32)
                sums.append((metas[k, 0, p], a, b))
            for at, a, b in sums:
                acc[at, :, own_cols] += a
                acc[at, :, other_cols] += b
            return carry

        lax.fori_loop(0, room // UNROLL, some, 0)


def first_kernel(sources, room, *refs):
    basis, mine, other = (refs[i * sources : (i + 1) * sources] for i in range(3))
    acc, staged, metas, sem = refs[3 * sources :]
    add_products(room, basis, basis, mine, other, acc, staged, metas, sem)


def last_kernel(room, blocks, rows, chunk, labels, basis, mine, other, before, *refs):
    keep_low, keep_high, send_low, send_high, acc, staged, metas, sem = refs
    held = slice(chunk * rows, (chunk + 1) * rows)
    add_products(room, [labels], [basis], [mine], [other], acc, staged, metas, sem)
    part = keep_low.shape[0]
    for i, out in enumerate((keep_low, keep_high, send_low, send_high)):
        for o in range(part):
            at = slice((i * part + o) * blocks, (i * part + o + 1) * blocks)
            out[o] = (before[at, held] + acc[at]).astype(out.dtype)


def combine_kernel(rows, border, start, bases, *refs):
    mine, other = refs[:2]
    counts = [len(each) for each in bases]
    addends, outs = refs[2 : 2 + sum(counts)], refs[2 + sum(counts) :]
    combined, sends = outs[0], outs[1:]
    core = lax.axis_index("mp")
    width = mine.shape[1]
    own_cols = pl.ds(pl.multiple_of(core * width, width), width)
    other_cols = pl.ds(pl.multiple_of((1 - core) * width, width), width)
    for chunk in range(CHUNKS):
        parts = addends[sum(counts[:chunk]) : sum(counts[: chunk + 1])]
        first = core * (rows * CHUNKS) + chunk * rows
        held_rows = slice(chunk * rows, (chunk + 1) * rows)
        for i in range(combined.shape[0]):
            b = start + i
            at = pl.ds(pl.multiple_of(b * BLK + first, rows), rows)
            for cols, held in ((own_cols, mine), (other_cols, other)):
                total = held[at, :].astype(jnp.float32)
                for part, base in zip(parts, bases[chunk]):
                    total = total + part[0, b - base, :, cols].astype(jnp.float32)
                combined[i, held_rows, cols] = total.astype(combined.dtype)
    if sends:
        odd = lax.axis_index("graph") % 2
        even_send, odd_send = sends
        even_send[...] = combined[pl.ds((1 - odd) * border, border)]
        odd_send[...] = combined[pl.ds(odd * border, border)]


def mlp_kernel(border, start, blocks, reverse, valid, combined, *refs):
    came, refs = (refs[:2], refs[2:]) if start == 0 else (None, refs)
    in_own, in_other, out_own, out_other, final_own, final_other, state = refs
    count, share, width = combined.shape
    core = lax.axis_index("mp")
    odd = lax.axis_index("graph") % 2 == 1
    first = core * share
    for i in range(count):
        b = start + i
        within = reverse[b] % blocks
        if came is None:
            pair = combined[within - start]
        else:
            w = jnp.clip(within - (border if b < border else 0), 0, border - 1)
            pair = jnp.where(odd == (b < border), came[0][w], came[1][w])
        state[i * share : (i + 1) * share] = (
            combined[i].astype(jnp.float32) + pair.astype(jnp.float32)
        ) * pair_scale
    for layer in range(MLPS):
        layer_input = state[...].astype(jnp.bfloat16)
        total = state[...]
        for w_in, w_out in ((in_own, out_own), (in_other, out_other)):
            value = jnp.dot(layer_input, w_in[layer], preferred_element_type=jnp.float32)
            hidden = (value / (1.0 + jnp.exp(-value))).astype(jnp.bfloat16)
            total = total + jnp.dot(hidden, w_out[layer], preferred_element_type=jnp.float32)
        state[...] = total
    half = width // 2
    own_cols = pl.ds(pl.multiple_of(core * half, half), half)
    other_cols = pl.ds(pl.multiple_of((1 - core) * half, half), half)
    row = lax.broadcasted_iota(jnp.int32, (share, half), 0) + first
    limit = valid[0]
    for i in range(count):
        keep = row + (start + i) * BLK < limit
        at = slice(i * share, (i + 1) * share)
        final_own[i] = jnp.where(keep, state[at, own_cols], 0.0).astype(final_own.dtype)
        final_other[i] = jnp.where(keep, state[at, other_cols], 0.0).astype(final_other.dtype)


def join_kernel(starts, *refs):
    parts = len(starts)
    own, came, out = refs[:parts], refs[parts : 2 * parts], refs[2 * parts]
    core = lax.axis_index("mp")
    for i, start in enumerate(starts):
        count, share, _ = own[i].shape
        for b in range(count):
            here = (start + b) * BLK + core * share
            there = (start + b) * BLK + (1 - core) * share
            out[pl.ds(pl.multiple_of(here, share), share), :] = own[i][b]
            out[pl.ds(pl.multiple_of(there, share), share), :] = came[i][b]


def local(
    messages,
    basis_blocks,
    source_block,
    target_owner,
    target_block,
    row_counts,
    reverse_block,
    valid_edges,
    weight_in,
    weight_out,
):
    devices = lax.axis_size("graph")
    edge_rows, part_width = messages.shape
    width = part_width * lax.axis_size("mp")
    blocks = edge_rows // BLK
    slots = source_block.shape[0]
    capacity = max(2, (slots + devices - 1) // devices + 1)
    border = blocks // 4
    near, far = split_bits(devices)
    groups = 1 << len(near)
    owners = devices // groups
    room = min(slots, capacity * owners)
    room = -(-room // UNROLL) * UNROLL
    rows = BLK // lax.axis_size("mp") // CHUNKS
    bf16 = jnp.bfloat16

    def near_send(array, k):
        return lax.ppermute(array, "graph", xor_pairs(devices, near_mask(near, k)))

    def far_send(array, bit):
        return lax.ppermute(array, "graph", xor_pairs(devices, 1 << bit))

    def swap(array):
        return lax.ppermute(array, "mp", [(0, 1), (1, 0)])

    mine = [messages, near_send(messages, 1), near_send(messages, 2)]
    other = [swap(messages)]
    in_other, out_other = swap(weight_in), swap(weight_out)

    share = rows * CHUNKS
    whole_shape = jax.ShapeDtypeStruct((room + 1, share, BLK), bf16)
    cut_shapes = [
        jax.ShapeDtypeStruct((room + (1 if j == 0 else 6), rows, BLK), bf16) for j in range(CHUNKS)
    ]
    packed = pl.pallas_call(
        functools.partial(pack_kernel, near, far, room, rows, blocks),
        out_shape=[whole_shape] * (groups - 1) + cut_shapes,
        in_specs=[smem()] * 4 + [full(None)],
        out_specs=[full(None)] * (groups - 1 + CHUNKS),
        scratch_shapes=[pltpu.SMEM((groups * room,), jnp.int32), pltpu.SMEM((groups,), jnp.int32)],
        compiler_params=grant(),
        cost_estimate=spent(6),
        name="pack",
    )(
        target_owner[:, 0],
        source_block,
        target_block,
        row_counts,
        after_all(basis_blocks, other[0], in_other, out_other),
    )
    last = groups - 1
    middle = edge_rows // 2
    basis = [packed[0]]
    for k in range(1, last):
        basis.append(near_send(after_all(packed[k], *mine[1:]), k))
    ready = [after_all(array, packed[0]) for array in mine[1:]]
    onward = [near_send(ready[0][:middle], 2), near_send(ready[1][middle:], 1)]
    mine.append(jnp.concatenate(onward, axis=0))
    other.extend(swap(after_all(array, *basis[1:])) for array in mine[1:])
    acc_shape = (owners * blocks, rows, width)
    acc_bytes = owners * blocks * rows * width * 4
    partial = pl.pallas_call(
        functools.partial(first_kernel, last, room),
        out_shape=jax.ShapeDtypeStruct((owners * blocks, share, width), jnp.float32),
        in_specs=[full(None)] * (3 * last),
        out_specs=full(None),
        scratch_shapes=[
            pltpu.VMEM((last, 16, BLK), jnp.int32),
            pltpu.SMEM((last, 16, BLK), jnp.int32),
            pltpu.SemaphoreType.DMA,
        ],
        compiler_params=grant(CHUNKS * acc_bytes),
        cost_estimate=spent(4),
        name="first_products",
    )(*basis[:last], *mine[:last], *other[:last])

    part_owners_shape = jax.ShapeDtypeStruct((owners // 4, blocks, rows, width), bf16)
    border_shape = jax.ShapeDtypeStruct((border, share, width), bf16)
    even_pairs = [(i, i ^ 1) for i in range(devices)]
    odd_pairs = [(i, (i + 1 if i % 2 else i - 1) % devices) for i in range(devices)]
    cut, waited, came_first = [], basis[1:], None
    sums, lows, highs = [], [], []
    for chunk in range(CHUNKS):
        cut.append(near_send(after_all(packed[last + chunk], *waited), last))
        waits = []
        keep_low, keep_high, send_low, send_high = pl.pallas_call(
            functools.partial(last_kernel, room, blocks, rows, chunk),
            out_shape=[part_owners_shape] * 4,
            in_specs=[full(None)] * 5,
            out_specs=[full(None)] * 4,
            scratch_shapes=[
                pltpu.VMEM(acc_shape, jnp.float32),
                pltpu.VMEM((1, 16, BLK), jnp.int32),
                pltpu.SMEM((1, 16, BLK), jnp.int32),
                pltpu.SemaphoreType.DMA,
            ],
            compiler_params=grant(4 * acc_bytes),
            cost_estimate=spent(2),
            name="last_products",
        )(cut[0], after_all(cut[chunk], *waits), mine[last], other[last], partial)
        waited = [partial]
        came = far_send(send_high, far[0])
        came_first = (keep_high.astype(jnp.float32) + came.astype(jnp.float32)).astype(bf16)
        sums.append(came_first)
        highs.append(came)
        lows.append((keep_low, send_low))
    lows = [
        (keep_low, far_send(after_all(send_low, came), far[0]))
        for (keep_low, send_low), came in zip(lows, highs)
    ]
    starts = [0, 2 * border]
    stops = [2 * border, blocks]
    arrived = []
    for chunk in range(CHUNKS):
        pieces = [(0, blocks)] if chunk < CHUNKS - 1 else list(zip(starts, stops))
        found = []
        for start, stop in pieces:
            send, addends, bases = sums[chunk][:, start:stop], list(lows[chunk]), [0, 0]
            if start > 0:
                send = after_all(send, arrived[0][0][0][-1])
            size = owners // 4
            for index, bit in enumerate(far[1:]):
                addends.append(far_send(send, bit))
                bases.append(start)
                if index + 2 < len(far):
                    size = size // 2
                    send = sum(
                        part[size : 2 * size, start - base : stop - base].astype(jnp.float32)
                        for part, base in zip(addends, bases)
                    ).astype(bf16)
            found.append((addends, tuple(bases)))
        arrived.append(found if len(found) > 1 else found * 2)
    finals, came = [], []
    for index, (start, stop) in enumerate(zip(starts, stops)):
        addends = [array for found in arrived for array in found[index][0]]
        bases = tuple(found[index][1] for found in arrived)
        piece_shape = jax.ShapeDtypeStruct((stop - start, share, width), bf16)
        part_shape = jax.ShapeDtypeStruct((stop - start, share, part_width), bf16)
        outs = pl.pallas_call(
            functools.partial(combine_kernel, rows, border, start, bases),
            out_shape=[piece_shape] + [border_shape] * (2 if start == 0 else 0),
            in_specs=[full(None)] * (2 + len(addends)),
            out_specs=[full(None)] * (3 if start == 0 else 1),
            compiler_params=grant(acc_bytes),
            cost_estimate=spent(0.5),
            name="combine",
        )(mine[0], other[0], *addends)
        if start == 0:
            came = [
                lax.ppermute(outs[2], "graph", odd_pairs),
                lax.ppermute(outs[1], "graph", even_pairs),
            ][::-1]
        operands = [outs[0]] + (came if start == 0 else [])
        own, theirs = pl.pallas_call(
            functools.partial(mlp_kernel, border, start, blocks),
            out_shape=[part_shape] * 2,
            in_specs=[smem()] * 2 + [full(None)] * (4 + len(operands)),
            out_specs=[full(None)] * 2,
            scratch_shapes=[pltpu.VMEM(((stop - start) * share, width), jnp.float32)],
            compiler_params=grant(),
            cost_estimate=spent(2),
            name="mlp",
        )(reverse_block, valid_edges, *operands, weight_in, in_other, weight_out, out_other)
        finals.append((own, swap(theirs)))

    return pl.pallas_call(
        functools.partial(join_kernel, starts),
        out_shape=jax.ShapeDtypeStruct(messages.shape, bf16),
        in_specs=[full(None)] * (2 * len(finals)),
        out_specs=full(None),
        compiler_params=grant(),
        cost_estimate=spent(1),
        name="join",
    )(*[own for own, _ in finals], *[theirs for _, theirs in finals])


def solution(mesh):
    in_specs = (
        P("graph", "mp"),
        P("graph", None, None),
        P("graph"),
        P("graph", None),
        P("graph"),
        P("graph"),
        P("graph"),
        P("graph"),
        P(None, None, "mp"),
        P(None, "mp", None),
    )
    out_specs = P("graph", "mp")
    return jax.shard_map(local, mesh=mesh, in_specs=in_specs, out_specs=out_specs, check_vma=False)
```

```python
import functools

import jax
import jax.numpy as jnp
from jax import lax
from jax.experimental import pallas as pl
from jax.experimental.pallas import tpu as pltpu
from jax.sharding import PartitionSpec as P

MLPS = 3
BLK = 128
CHUNKS = 2
UNROLL = 14
GRANT = 12 * 1024 * 1024

pair_scale = 0.7071067811865476


def split_bits(devices):
    count = devices.bit_length() - 1
    near = [bit for bit in (0, 2) if bit < count]
    far = [bit for bit in range(count) if bit not in near]
    return near, far


def xor_pairs(devices, mask):
    return [(i, i ^ mask) for i in range(devices)]


def near_mask(near, k):
    return sum(((k >> i) & 1) << bit for i, bit in enumerate(near))


def grant(extra=0):
    return pltpu.CompilerParams(vmem_limit_bytes=GRANT + extra)


def spent(microseconds):
    return pl.CostEstimate(
        flops=0, bytes_accessed=int(microseconds * 3.69e6), transcendentals=0
    )


def after_all(value, *others):
    if not others:
        return value
    return lax.optimization_barrier((value, *others))[0]


def full(shape):
    return pl.BlockSpec(memory_space=pltpu.VMEM)


def smem():
    return pl.BlockSpec(memory_space=pltpu.SMEM)


def pack_kernel(near, far, room, rows, blocks, owner, source, target, counts, basis, *refs):
    groups = 1 << len(near)
    whole, cut = refs[: groups - 1], refs[groups - 1 : groups - 1 + CHUNKS]
    table, fill = refs[groups - 1 + CHUNKS :]
    slots = basis.shape[0]
    me = lax.axis_index("graph")
    core = lax.axis_index("mp")
    for k in range(groups):
        fill[k] = 0

    def clear(i, carry):
        table[i] = -1
        return carry

    lax.fori_loop(0, groups * room, clear, 0, unroll=4)

    def route(t, carry):
        rel = owner[t] ^ me
        k = 0
        for i, bit in enumerate(near):
            k = k + (((rel >> bit) & 1) << i)
        p = fill[k]
        fill[k] = p + 1
        table[k * room + p] = t
        return carry

    lax.fori_loop(0, slots, route, 0)

    share = rows * CHUNKS
    first = core * share
    row = lax.broadcasted_iota(jnp.int32, (share, BLK), 0)
    label_row = lax.broadcasted_iota(jnp.int32, (rows, BLK), 0)
    lane = lax.broadcasted_iota(jnp.int32, (rows, BLK), 1)
    for k in range(groups):

        def one(p, labels):
            t = table[k * room + p]
            there = t >= 0
            s = jnp.maximum(t, 0)
            rel = owner[s] ^ me
            b = 0
            for i, bit in enumerate(far):
                b = b + (((rel >> bit) & 1) << (len(far) - 1 - i))
            place = jnp.where(there, b * blocks + target[s], 0)
            place = jnp.where(label_row == 0, place, source[s])
            labels = jnp.where(lane == p, place, labels)
            count = jnp.where(there, counts[s], 0)
            block = basis[s, pl.ds(pl.multiple_of(first, share), share), :]
            block = jnp.where(row + first < count, block, jnp.zeros_like(block))
            if k < groups - 1:
                whole[k][p] = block
            else:
                for j in range(CHUNKS):
                    cut[j][p] = block[j * rows : (j + 1) * rows]
            return labels

        labels = lax.fori_loop(0, room, one, jnp.zeros((rows, BLK), jnp.int32), unroll=2)
        labels = labels.astype(jnp.float32).astype(jnp.bfloat16)
        if k < groups - 1:
            whole[k][room, :rows] = labels
        else:
            cut[0][room] = labels


def add_products(room, labels, basis, mine, other, acc, staged, metas, sem):
    sources = len(basis)
    core = lax.axis_index("mp")
    width = mine[0].shape[1]
    own_cols = pl.ds(pl.multiple_of(core * width, width), width)
    other_cols = pl.ds(pl.multiple_of((1 - core) * width, width), width)
    for k in range(sources):
        staged[k] = labels[k][room, :16, :].astype(jnp.float32).astype(jnp.int32)
    copy = pltpu.make_async_copy(staged, metas, sem)
    copy.start()
    acc[...] = jnp.zeros_like(acc)
    copy.wait()
    for k in range(sources):

        def some(step, carry):
            sums = []
            for u in range(UNROLL):
                p = step * UNROLL + u
                s = metas[k, 1, p]
                at = pl.ds(pl.multiple_of(s * BLK, BLK), BLK)
                left = basis[k][p]
                a = jnp.dot(left, mine[k][at, :], preferred_element_type=jnp.float32)
                b = jnp.dot(left, other[k][at, :], preferred_element_type=jnp.float32)
                sums.append((metas[k, 0, p], a, b))
            for at, a, b in sums:
                acc[at, :, own_cols] += a
                acc[at, :, other_cols] += b
            return carry

        lax.fori_loop(0, room // UNROLL, some, 0)


def first_kernel(sources, room, *refs):
    basis, mine, other = (refs[i * sources : (i + 1) * sources] for i in range(3))
    acc, staged, metas, sem = refs[3 * sources :]
    add_products(room, basis, basis, mine, other, acc, staged, metas, sem)


def last_kernel(room, blocks, rows, chunk, labels, basis, mine, other, before, *refs):
    keep_low, keep_high, send_low, send_high, acc, staged, metas, sem = refs
    held = slice(chunk * rows, (chunk + 1) * rows)
    add_products(room, [labels], [basis], [mine], [other], acc, staged, metas, sem)
    part = keep_low.shape[0]
    for i, out in enumerate((keep_low, keep_high, send_low, send_high)):
        for o in range(part):
            at = slice((i * part + o) * blocks, (i * part + o + 1) * blocks)
            out[o] = (before[at, held] + acc[at]).astype(out.dtype)


def combine_kernel(rows, border, start, bases, *refs):
    mine, other = refs[:2]
    counts = [len(each) for each in bases]
    addends, outs = refs[2 : 2 + sum(counts)], refs[2 + sum(counts) :]
    combined, sends = outs[0], outs[1:]
    core = lax.axis_index("mp")
    width = mine.shape[1]
    own_cols = pl.ds(pl.multiple_of(core * width, width), width)
    other_cols = pl.ds(pl.multiple_of((1 - core) * width, width), width)
    for chunk in range(CHUNKS):
        parts = addends[sum(counts[:chunk]) : sum(counts[: chunk + 1])]
        first = core * (rows * CHUNKS) + chunk * rows
        held_rows = slice(chunk * rows, (chunk + 1) * rows)
        for i in range(combined.shape[0]):
            b = start + i
            at = pl.ds(pl.multiple_of(b * BLK + first, rows), rows)
            for cols, held in ((own_cols, mine), (other_cols, other)):
                total = held[at, :].astype(jnp.float32)
                for part, base in zip(parts, bases[chunk]):
                    total = total + part[0, b - base, :, cols].astype(jnp.float32)
                combined[i, held_rows, cols] = total.astype(combined.dtype)
    if sends:
        odd = lax.axis_index("graph") % 2
        even_send, odd_send = sends
        even_send[...] = combined[pl.ds((1 - odd) * border, border)]
        odd_send[...] = combined[pl.ds(odd * border, border)]


def mlp_kernel(border, start, blocks, reverse, valid, combined, *refs):
    came, refs = (refs[:2], refs[2:]) if start == 0 else (None, refs)
    in_own, in_other, out_own, out_other, final_own, final_other, state = refs
    count, share, width = combined.shape
    core = lax.axis_index("mp")
    odd = lax.axis_index("graph") % 2 == 1
    first = core * share
    for i in range(count):
        b = start + i
        within = reverse[b] % blocks
        if came is None:
            pair = combined[within - start]
        else:
            w = jnp.clip(within - (border if b < border else 0), 0, border - 1)
            pair = jnp.where(odd == (b < border), came[0][w], came[1][w])
        state[i * share : (i + 1) * share] = (
            combined[i].astype(jnp.float32) + pair.astype(jnp.float32)
        ) * pair_scale
    for layer in range(MLPS):
        layer_input = state[...].astype(jnp.bfloat16)
        total = state[...]
        for w_in, w_out in ((in_own, out_own), (in_other, out_other)):
            value = jnp.dot(layer_input, w_in[layer], preferred_element_type=jnp.float32)
            hidden = (value / (1.0 + jnp.exp(-value))).astype(jnp.bfloat16)
            total = total + jnp.dot(hidden, w_out[layer], preferred_element_type=jnp.float32)
        state[...] = total
    half = width // 2
    own_cols = pl.ds(pl.multiple_of(core * half, half), half)
    other_cols = pl.ds(pl.multiple_of((1 - core) * half, half), half)
    row = lax.broadcasted_iota(jnp.int32, (share, half), 0) + first
    limit = valid[0]
    for i in range(count):
        keep = row + (start + i) * BLK < limit
        at = slice(i * share, (i + 1) * share)
        final_own[i] = jnp.where(keep, state[at, own_cols], 0.0).astype(final_own.dtype)
        final_other[i] = jnp.where(keep, state[at, other_cols], 0.0).astype(final_other.dtype)


def join_kernel(starts, *refs):
    parts = len(starts)
    own, came, out = refs[:parts], refs[parts : 2 * parts], refs[2 * parts]
    core = lax.axis_index("mp")
    for i, start in enumerate(starts):
        count, share, _ = own[i].shape
        for b in range(count):
            here = (start + b) * BLK + core * share
            there = (start + b) * BLK + (1 - core) * share
            out[pl.ds(pl.multiple_of(here, share), share), :] = own[i][b]
            out[pl.ds(pl.multiple_of(there, share), share), :] = came[i][b]


def local(
    messages,
    basis_blocks,
    source_block,
    target_owner,
    target_block,
    row_counts,
    reverse_block,
    valid_edges,
    weight_in,
    weight_out,
):
    devices = lax.axis_size("graph")
    edge_rows, part_width = messages.shape
    width = part_width * lax.axis_size("mp")
    blocks = edge_rows // BLK
    slots = source_block.shape[0]
    capacity = max(2, (slots + devices - 1) // devices + 1)
    border = blocks // 4
    near, far = split_bits(devices)
    groups = 1 << len(near)
    owners = devices // groups
    room = min(slots, capacity * owners)
    room = -(-room // UNROLL) * UNROLL
    rows = BLK // lax.axis_size("mp") // CHUNKS
    bf16 = jnp.bfloat16

    def near_send(array, k):
        return lax.ppermute(array, "graph", xor_pairs(devices, near_mask(near, k)))

    def far_send(array, bit):
        return lax.ppermute(array, "graph", xor_pairs(devices, 1 << bit))

    def swap(array):
        return lax.ppermute(array, "mp", [(0, 1), (1, 0)])

    mine = [messages, near_send(messages, 1), near_send(messages, 2)]
    in_other, out_other = swap(weight_in), swap(weight_out)

    share = rows * CHUNKS
    whole_shape = jax.ShapeDtypeStruct((room + 1, share, BLK), bf16)
    cut_shapes = [
        jax.ShapeDtypeStruct((room + (1 if j == 0 else 6), rows, BLK), bf16) for j in range(CHUNKS)
    ]
    packed = pl.pallas_call(
        functools.partial(pack_kernel, near, far, room, rows, blocks),
        out_shape=[whole_shape] * (groups - 1) + cut_shapes,
        in_specs=[smem()] * 4 + [full(None)],
        out_specs=[full(None)] * (groups - 1 + CHUNKS),
        scratch_shapes=[pltpu.SMEM((groups * room,), jnp.int32), pltpu.SMEM((groups,), jnp.int32)],
        compiler_params=grant(),
        cost_estimate=spent(6),
        name="pack",
    )(
        target_owner[:, 0],
        source_block,
        target_block,
        row_counts,
        after_all(basis_blocks, in_other, out_other),
    )
    last = groups - 1
    middle = edge_rows // 2
    other = [swap(after_all(messages, packed[0]))]
    basis = [packed[0]]
    for k in range(1, last):
        basis.append(near_send(packed[k], k))
    ready = [after_all(array, packed[0]) for array in mine[1:]]
    onward = [near_send(ready[0][:middle], 2), near_send(ready[1][middle:], 1)]
    mine.append(jnp.concatenate(onward, axis=0))
    other.extend(swap(after_all(array, *basis[1:])) for array in mine[1:])
    acc_shape = (owners * blocks, rows, width)
    acc_bytes = owners * blocks * rows * width * 4
    partial = pl.pallas_call(
        functools.partial(first_kernel, last, room),
        out_shape=jax.ShapeDtypeStruct((owners * blocks, share, width), jnp.float32),
        in_specs=[full(None)] * (3 * last),
        out_specs=full(None),
        scratch_shapes=[
            pltpu.VMEM((last, 16, BLK), jnp.int32),
            pltpu.SMEM((last, 16, BLK), jnp.int32),
            pltpu.SemaphoreType.DMA,
        ],
        compiler_params=grant(CHUNKS * acc_bytes),
        cost_estimate=spent(4),
        name="first_products",
    )(*basis[:last], *mine[:last], *other[:last])

    part_owners_shape = jax.ShapeDtypeStruct((owners // 4, blocks, rows, width), bf16)
    border_shape = jax.ShapeDtypeStruct((border, share, width), bf16)
    even_pairs = [(i, i ^ 1) for i in range(devices)]
    odd_pairs = [(i, (i + 1 if i % 2 else i - 1) % devices) for i in range(devices)]
    cut, waited, came_first = [], basis[1:], None
    sums, lows, highs = [], [], []
    for chunk in range(CHUNKS):
        cut.append(near_send(after_all(packed[last + chunk], *waited), last))
        waits = []
        keep_low, keep_high, send_low, send_high = pl.pallas_call(
            functools.partial(last_kernel, room, blocks, rows, chunk),
            out_shape=[part_owners_shape] * 4,
            in_specs=[full(None)] * 5,
            out_specs=[full(None)] * 4,
            scratch_shapes=[
                pltpu.VMEM(acc_shape, jnp.float32),
                pltpu.VMEM((1, 16, BLK), jnp.int32),
                pltpu.SMEM((1, 16, BLK), jnp.int32),
                pltpu.SemaphoreType.DMA,
            ],
            compiler_params=grant(4 * acc_bytes),
            cost_estimate=spent(2),
            name="last_products",
        )(cut[0], after_all(cut[chunk], *waits), mine[last], other[last], partial)
        waited = [partial]
        came = far_send(send_high, far[0])
        came_first = (keep_high.astype(jnp.float32) + came.astype(jnp.float32)).astype(bf16)
        sums.append(came_first)
        highs.append(came)
        lows.append((keep_low, send_low))
    lows = [
        (keep_low, far_send(after_all(send_low, highs[-1]), far[0]))
        for (keep_low, send_low), came in zip(lows, highs)
    ]
    starts = [0, 2 * border]
    stops = [2 * border, blocks]
    arrived = []
    for chunk in range(CHUNKS):
        pieces = [(0, blocks)] if chunk < CHUNKS - 1 else list(zip(starts, stops))
        found = []
        for start, stop in pieces:
            send, addends, bases = sums[chunk][:, start:stop], list(lows[chunk]), [0, 0]
            if start > 0:
                send = after_all(send, arrived[0][0][0][-1])
            size = owners // 4
            for index, bit in enumerate(far[1:]):
                addends.append(far_send(send, bit))
                bases.append(start)
                if index + 2 < len(far):
                    size = size // 2
                    send = sum(
                        part[size : 2 * size, start - base : stop - base].astype(jnp.float32)
                        for part, base in zip(addends, bases)
                    ).astype(bf16)
            found.append((addends, tuple(bases)))
        arrived.append(found if len(found) > 1 else found * 2)
    finals, came = [], []
    for index, (start, stop) in enumerate(zip(starts, stops)):
        addends = [array for found in arrived for array in found[index][0]]
        bases = tuple(found[index][1] for found in arrived)
        piece_shape = jax.ShapeDtypeStruct((stop - start, share, width), bf16)
        part_shape = jax.ShapeDtypeStruct((stop - start, share, part_width), bf16)
        outs = pl.pallas_call(
            functools.partial(combine_kernel, rows, border, start, bases),
            out_shape=[piece_shape] + [border_shape] * (2 if start == 0 else 0),
            in_specs=[full(None)] * (2 + len(addends)),
            out_specs=[full(None)] * (3 if start == 0 else 1),
            compiler_params=grant(acc_bytes),
            cost_estimate=spent(0.5),
            name="combine",
        )(mine[0], other[0], *addends)
        if start == 0:
            came = [
                lax.ppermute(outs[2], "graph", odd_pairs),
                lax.ppermute(outs[1], "graph", even_pairs),
            ][::-1]
        operands = [outs[0]] + (came if start == 0 else [])
        own, theirs = pl.pallas_call(
            functools.partial(mlp_kernel, border, start, blocks),
            out_shape=[part_shape] * 2,
            in_specs=[smem()] * 2 + [full(None)] * (4 + len(operands)),
            out_specs=[full(None)] * 2,
            scratch_shapes=[pltpu.VMEM(((stop - start) * share, width), jnp.float32)],
            compiler_params=grant(),
            cost_estimate=spent(2),
            name="mlp",
        )(reverse_block, valid_edges, *operands, weight_in, in_other, weight_out, out_other)
        finals.append((own, swap(theirs)))

    return pl.pallas_call(
        functools.partial(join_kernel, starts),
        out_shape=jax.ShapeDtypeStruct(messages.shape, bf16),
        in_specs=[full(None)] * (2 * len(finals)),
        out_specs=full(None),
        compiler_params=grant(),
        cost_estimate=spent(1),
        name="join",
    )(*[own for own, _ in finals], *[theirs for _, theirs in finals])


def solution(mesh):
    in_specs = (
        P("graph", "mp"),
        P("graph", None, None),
        P("graph"),
        P("graph", None),
        P("graph"),
        P("graph"),
        P("graph"),
        P("graph"),
        P(None, None, "mp"),
        P(None, "mp", None),
    )
    out_specs = P("graph", "mp")
    return jax.shard_map(local, mesh=mesh, in_specs=in_specs, out_specs=out_specs, check_vma=False)
```

```python
import functools

import jax
import jax.numpy as jnp
from jax import lax
from jax.experimental import pallas as pl
from jax.experimental.pallas import tpu as pltpu
from jax.sharding import PartitionSpec as P

MLPS = 3
BLK = 128
CHUNKS = 2
UNROLL = 28
LABEL_ROWS = 16
SPARE = 6
GRANT = 12 * 1024 * 1024

pair_scale = 0.7071067811865476


def split_bits(devices):
    count = devices.bit_length() - 1
    near = [bit for bit in (0, 2) if bit < count]
    far = [bit for bit in range(count) if bit not in near]
    return near, far


def xor_pairs(devices, mask):
    return [(i, i ^ mask) for i in range(devices)]


def near_mask(near, k):
    return sum(((k >> i) & 1) << bit for i, bit in enumerate(near))


def grant(extra=0):
    return pltpu.CompilerParams(vmem_limit_bytes=GRANT + extra)


def spent(microseconds):
    return pl.CostEstimate(
        flops=0, bytes_accessed=int(microseconds * 3.69e6), transcendentals=0
    )


def after_all(value, *others):
    if not others:
        return value
    return lax.optimization_barrier((value, *others))[0]


def full(shape):
    return pl.BlockSpec(memory_space=pltpu.VMEM)


def smem():
    return pl.BlockSpec(memory_space=pltpu.SMEM)


def pack_kernel(near, far, room, rows, blocks, owner, source, target, counts, basis, *refs):
    groups = 1 << len(near)
    whole, cut = refs[: groups - 1], refs[groups - 1 : groups - 1 + CHUNKS]
    table, fill = refs[groups - 1 + CHUNKS :]
    slots = basis.shape[0]
    me = lax.axis_index("graph")
    core = lax.axis_index("mp")
    for k in range(groups):
        fill[k] = 0

    def clear(i, carry):
        table[i] = -1
        return carry

    lax.fori_loop(0, groups * room, clear, 0, unroll=4)

    def route(t, carry):
        rel = owner[t] ^ me
        k = 0
        for i, bit in enumerate(near):
            k = k + (((rel >> bit) & 1) << i)
        p = fill[k]
        fill[k] = p + 1
        table[k * room + p] = t
        return carry

    lax.fori_loop(0, slots, route, 0)

    share = rows * CHUNKS
    first = core * share
    row = lax.broadcasted_iota(jnp.int32, (share, BLK), 0)
    label_row = lax.broadcasted_iota(jnp.int32, (LABEL_ROWS, BLK), 0)
    lane = lax.broadcasted_iota(jnp.int32, (LABEL_ROWS, BLK), 1)
    for k in range(groups):

        def one(p, labels):
            t = table[k * room + p]
            there = t >= 0
            s = jnp.maximum(t, 0)
            rel = owner[s] ^ me
            b = 0
            for i, bit in enumerate(far):
                b = b + (((rel >> bit) & 1) << (len(far) - 1 - i))
            place = jnp.where(there, b * blocks + target[s], 0)
            place = jnp.where(label_row == 0, place, source[s])
            labels = jnp.where(lane == p, place, labels)
            count = jnp.where(there, counts[s], 0)
            block = basis[s, pl.ds(pl.multiple_of(first, share), share), :]
            block = jnp.where(row + first < count, block, jnp.zeros_like(block))
            if k < groups - 1:
                whole[k][pl.ds(pl.multiple_of(p * share, share), share), :] = block
            else:
                for j in range(CHUNKS):
                    at = pl.ds(pl.multiple_of(p * rows, rows), rows)
                    cut[j][at, :] = block[j * rows : (j + 1) * rows]
            return labels

        labels = lax.fori_loop(0, room, one, jnp.zeros((LABEL_ROWS, BLK), jnp.int32), unroll=2)
        labels = labels.astype(jnp.float32).astype(jnp.bfloat16)
        if k < groups - 1:
            whole[k][room * share :, :] = labels
        else:
            cut[0][room * rows :, :] = labels


def add_products(room, height, labels, basis, mine, other, acc, staged, metas, sem):
    sources = len(basis)
    core = lax.axis_index("mp")
    width = mine[0].shape[1]
    own_cols = pl.ds(pl.multiple_of(core * width, width), width)
    other_cols = pl.ds(pl.multiple_of((1 - core) * width, width), width)
    for k in range(sources):
        staged[k] = labels[k][room * height :, :].astype(jnp.float32).astype(jnp.int32)[:8]
    copy = pltpu.make_async_copy(staged, metas, sem)
    copy.start()
    acc[...] = jnp.zeros_like(acc)
    copy.wait()
    for k in range(sources):

        def some(step, carry):
            sums = []
            for u in range(UNROLL):
                p = step * UNROLL + u
                s = metas[k, 1, p]
                at = pl.ds(pl.multiple_of(s * BLK, BLK), BLK)
                left = basis[k][pl.ds(pl.multiple_of(p * height, height), height), :]
                a = jnp.dot(left, mine[k][at, :], preferred_element_type=jnp.float32)
                b = jnp.dot(left, other[k][at, :], preferred_element_type=jnp.float32)
                sums.append((metas[k, 0, p], a, b))
            for at, a, b in sums:
                acc[at, :, own_cols] += a
                acc[at, :, other_cols] += b
            return carry

        lax.fori_loop(0, room // UNROLL, some, 0)


def first_kernel(sources, room, *refs):
    basis, mine, other = (refs[i * sources : (i + 1) * sources] for i in range(3))
    acc, staged, metas, sem = refs[3 * sources :]
    height = (basis[0].shape[0] - LABEL_ROWS) // room
    add_products(room, height, basis, basis, mine, other, acc, staged, metas, sem)


def last_kernel(room, blocks, rows, chunk, labels, basis, mine, other, before, *refs):
    keep_low, keep_high, send_low, send_high, acc, staged, metas, sem = refs
    held = slice(chunk * rows, (chunk + 1) * rows)
    add_products(room, rows, [labels], [basis], [mine], [other], acc, staged, metas, sem)
    part = keep_low.shape[0]
    for i, out in enumerate((keep_low, keep_high, send_low, send_high)):
        for o in range(part):
            at = slice((i * part + o) * blocks, (i * part + o + 1) * blocks)
            out[o] = (before[at, held] + acc[at]).astype(out.dtype)


def combine_kernel(rows, border, start, bases, *refs):
    mine, other = refs[:2]
    counts = [len(each) for each in bases]
    addends, outs = refs[2 : 2 + sum(counts)], refs[2 + sum(counts) :]
    combined, sends = outs[0], outs[1:]
    core = lax.axis_index("mp")
    width = mine.shape[1]
    own_cols = pl.ds(pl.multiple_of(core * width, width), width)
    other_cols = pl.ds(pl.multiple_of((1 - core) * width, width), width)
    for chunk in range(CHUNKS):
        parts = addends[sum(counts[:chunk]) : sum(counts[: chunk + 1])]
        first = core * (rows * CHUNKS) + chunk * rows
        held_rows = slice(chunk * rows, (chunk + 1) * rows)
        for i in range(combined.shape[0]):
            b = start + i
            at = pl.ds(pl.multiple_of(b * BLK + first, rows), rows)
            for cols, held in ((own_cols, mine), (other_cols, other)):
                total = held[at, :].astype(jnp.float32)
                for part, base in zip(parts, bases[chunk]):
                    total = total + part[0, b - base, :, cols].astype(jnp.float32)
                combined[i, held_rows, cols] = total.astype(combined.dtype)
    if sends:
        odd = lax.axis_index("graph") % 2
        even_send, odd_send = sends
        even_send[...] = combined[pl.ds((1 - odd) * border, border)]
        odd_send[...] = combined[pl.ds(odd * border, border)]


def mlp_kernel(border, start, blocks, reverse, valid, combined, *refs):
    came, refs = (refs[:2], refs[2:]) if start == 0 else (None, refs)
    in_own, in_other, out_own, out_other, final_own, final_other, state = refs
    count, share, width = combined.shape
    core = lax.axis_index("mp")
    odd = lax.axis_index("graph") % 2 == 1
    first = core * share
    for i in range(count):
        b = start + i
        within = reverse[b] % blocks
        if came is None:
            pair = combined[jnp.clip(within - start, 0, count - 1)]
        else:
            w = jnp.clip(within - (border if b < border else 0), 0, border - 1)
            pair = jnp.where(odd == (b < border), came[0][w], came[1][w])
        state[i * share : (i + 1) * share] = (
            combined[i].astype(jnp.float32) + pair.astype(jnp.float32)
        ) * pair_scale
    for layer in range(MLPS):
        layer_input = state[...].astype(jnp.bfloat16)
        total = state[...]
        for w_in, w_out in ((in_own, out_own), (in_other, out_other)):
            value = jnp.dot(layer_input, w_in[layer], preferred_element_type=jnp.float32)
            hidden = (0.5 * value * (1.0 + jnp.tanh(0.5 * value))).astype(jnp.bfloat16)
            total = total + jnp.dot(hidden, w_out[layer], preferred_element_type=jnp.float32)
        state[...] = total
    half = width // 2
    own_cols = pl.ds(pl.multiple_of(core * half, half), half)
    other_cols = pl.ds(pl.multiple_of((1 - core) * half, half), half)
    row = lax.broadcasted_iota(jnp.int32, (share, half), 0) + first
    limit = valid[0]
    for i in range(count):
        keep = row + (start + i) * BLK < limit
        at = slice(i * share, (i + 1) * share)
        final_own[i] = jnp.where(keep, state[at, own_cols], 0.0).astype(final_own.dtype)
        final_other[i] = jnp.where(keep, state[at, other_cols], 0.0).astype(final_other.dtype)


def join_kernel(starts, *refs):
    parts = len(starts)
    own, came, out = refs[:parts], refs[parts : 2 * parts], refs[2 * parts]
    core = lax.axis_index("mp")
    for i, start in enumerate(starts):
        count, share, _ = own[i].shape
        for b in range(count):
            here = (start + b) * BLK + core * share
            there = (start + b) * BLK + (1 - core) * share
            out[pl.ds(pl.multiple_of(here, share), share), :] = own[i][b]
            out[pl.ds(pl.multiple_of(there, share), share), :] = came[i][b]


def local(
    messages,
    basis_blocks,
    source_block,
    target_owner,
    target_block,
    row_counts,
    reverse_block,
    valid_edges,
    weight_in,
    weight_out,
):
    devices = lax.axis_size("graph")
    edge_rows, part_width = messages.shape
    width = part_width * lax.axis_size("mp")
    blocks = edge_rows // BLK
    slots = source_block.shape[0]
    capacity = max(2, (slots + devices - 1) // devices + 1)
    border = blocks // 4
    near, far = split_bits(devices)
    groups = 1 << len(near)
    owners = devices // groups
    room = min(slots, capacity * owners)
    room = -(-room // UNROLL) * UNROLL
    rows = BLK // lax.axis_size("mp") // CHUNKS
    bf16 = jnp.bfloat16

    def near_send(array, k):
        return lax.ppermute(array, "graph", xor_pairs(devices, near_mask(near, k)))

    def far_send(array, bit):
        return lax.ppermute(array, "graph", xor_pairs(devices, 1 << bit))

    def swap(array):
        return lax.ppermute(array, "mp", [(0, 1), (1, 0)])

    mine = [messages, near_send(messages, 1), near_send(messages, 2)]
    in_other, out_other = swap(weight_in), swap(weight_out)

    share = rows * CHUNKS
    whole_shape = jax.ShapeDtypeStruct((room * share + LABEL_ROWS, BLK), bf16)
    cut_shapes = [
        jax.ShapeDtypeStruct((room * rows + (LABEL_ROWS if j == 0 else SPARE * rows), BLK), bf16)
        for j in range(CHUNKS)
    ]
    packed = pl.pallas_call(
        functools.partial(pack_kernel, near, far, room, rows, blocks),
        out_shape=[whole_shape] * (groups - 1) + cut_shapes,
        in_specs=[smem()] * 4 + [full(None)],
        out_specs=[full(None)] * (groups - 1 + CHUNKS),
        scratch_shapes=[pltpu.SMEM((groups * room,), jnp.int32), pltpu.SMEM((groups,), jnp.int32)],
        compiler_params=grant(),
        cost_estimate=spent(6),
        name="pack",
    )(
        target_owner[:, 0],
        source_block,
        target_block,
        row_counts,
        after_all(basis_blocks, in_other, out_other),
    )
    last = groups - 1
    middle = edge_rows // 2
    other = [swap(after_all(messages, packed[0]))]
    basis = [packed[0]]
    for k in range(1, last):
        basis.append(near_send(packed[k], k))
    ready = [after_all(array, packed[0]) for array in mine[1:]]
    onward = [near_send(ready[0][:middle], 2), near_send(ready[1][middle:], 1)]
    mine.append(jnp.concatenate(onward, axis=0))
    other.extend(swap(after_all(array, *basis[1:])) for array in mine[1:])
    acc_shape = (owners * blocks, rows, width)
    acc_bytes = owners * blocks * rows * width * 4
    partial = pl.pallas_call(
        functools.partial(first_kernel, last, room),
        out_shape=jax.ShapeDtypeStruct((owners * blocks, share, width), jnp.float32),
        in_specs=[full(None)] * (3 * last),
        out_specs=full(None),
        scratch_shapes=[
            pltpu.VMEM((last, 8, BLK), jnp.int32),
            pltpu.SMEM((last, 8, BLK), jnp.int32),
            pltpu.SemaphoreType.DMA,
        ],
        compiler_params=grant(CHUNKS * acc_bytes),
        cost_estimate=spent(4),
        name="first_products",
    )(*basis[:last], *mine[:last], *other[:last])

    part_owners_shape = jax.ShapeDtypeStruct((owners // 4, blocks, rows, width), bf16)
    border_shape = jax.ShapeDtypeStruct((border, share, width), bf16)
    even_pairs = [(i, i ^ 1) for i in range(devices)]
    odd_pairs = [(i, (i + 1 if i % 2 else i - 1) % devices) for i in range(devices)]
    cut, waited = [], basis[1:]
    sums, lows, highs = [], [], []
    for chunk in range(CHUNKS):
        cut.append(near_send(after_all(packed[last + chunk], *waited), last))
        keep_low, keep_high, send_low, send_high = pl.pallas_call(
            functools.partial(last_kernel, room, blocks, rows, chunk),
            out_shape=[part_owners_shape] * 4,
            in_specs=[full(None)] * 5,
            out_specs=[full(None)] * 4,
            scratch_shapes=[
                pltpu.VMEM(acc_shape, jnp.float32),
                pltpu.VMEM((1, 8, BLK), jnp.int32),
                pltpu.SMEM((1, 8, BLK), jnp.int32),
                pltpu.SemaphoreType.DMA,
            ],
            compiler_params=grant(4 * acc_bytes),
            cost_estimate=spent(2),
            name="last_products",
        )(cut[0], cut[chunk], mine[last], other[last], partial)
        waited = [partial]
        came = far_send(send_high, far[0])
        sums.append((keep_high.astype(jnp.float32) + came.astype(jnp.float32)).astype(bf16))
        highs.append(came)
        lows.append((keep_low, send_low))
    lows = [
        (keep_low, far_send(after_all(send_low, highs[-1]), far[0]))
        for keep_low, send_low in lows
    ]
    starts = [0, 2 * border]
    stops = [2 * border, blocks]
    arrived = []
    for chunk in range(CHUNKS):
        pieces = [(0, blocks)] if chunk < CHUNKS - 1 else list(zip(starts, stops))
        found = []
        for start, stop in pieces:
            send, addends, bases = sums[chunk][:, start:stop], list(lows[chunk]), [0, 0]
            if start > 0:
                send = after_all(send, arrived[0][0][0][-1])
            size = owners // 4
            for index, bit in enumerate(far[1:]):
                addends.append(far_send(send, bit))
                bases.append(start)
                if index + 2 < len(far):
                    size = size // 2
                    send = sum(
                        part[size : 2 * size, start - base : stop - base].astype(jnp.float32)
                        for part, base in zip(addends, bases)
                    ).astype(bf16)
            found.append((addends, tuple(bases)))
        arrived.append(found if len(found) > 1 else found * 2)
    finals, came = [], []
    for index, (start, stop) in enumerate(zip(starts, stops)):
        addends = [array for found in arrived for array in found[index][0]]
        bases = tuple(found[index][1] for found in arrived)
        piece_shape = jax.ShapeDtypeStruct((stop - start, share, width), bf16)
        part_shape = jax.ShapeDtypeStruct((stop - start, share, part_width), bf16)
        outs = pl.pallas_call(
            functools.partial(combine_kernel, rows, border, start, bases),
            out_shape=[piece_shape] + [border_shape] * (2 if start == 0 else 0),
            in_specs=[full(None)] * (2 + len(addends)),
            out_specs=[full(None)] * (3 if start == 0 else 1),
            compiler_params=grant(acc_bytes),
            cost_estimate=spent(0.5),
            name="combine",
        )(mine[0], other[0], *addends)
        if start == 0:
            came = [
                lax.ppermute(outs[2], "graph", odd_pairs),
                lax.ppermute(outs[1], "graph", even_pairs),
            ][::-1]
        operands = [outs[0]] + (came if start == 0 else [])
        own, theirs = pl.pallas_call(
            functools.partial(mlp_kernel, border, start, blocks),
            out_shape=[part_shape] * 2,
            in_specs=[smem()] * 2 + [full(None)] * (4 + len(operands)),
            out_specs=[full(None)] * 2,
            scratch_shapes=[pltpu.VMEM(((stop - start) * share, width), jnp.float32)],
            compiler_params=grant(),
            cost_estimate=spent(2),
            name="mlp",
        )(reverse_block, valid_edges, *operands, weight_in, in_other, weight_out, out_other)
        finals.append((own, swap(theirs)))

    return pl.pallas_call(
        functools.partial(join_kernel, starts),
        out_shape=jax.ShapeDtypeStruct(messages.shape, bf16),
        in_specs=[full(None)] * (2 * len(finals)),
        out_specs=full(None),
        compiler_params=grant(),
        cost_estimate=spent(1),
        name="join",
    )(*[own for own, _ in finals], *[theirs for _, theirs in finals])


def solution(mesh):
    in_specs = (
        P("graph", "mp"),
        P("graph", None, None),
        P("graph"),
        P("graph", None),
        P("graph"),
        P("graph"),
        P("graph"),
        P("graph"),
        P(None, None, "mp"),
        P(None, "mp", None),
    )
    out_specs = P("graph", "mp")
    return jax.shard_map(local, mesh=mesh, in_specs=in_specs, out_specs=out_specs, check_vma=False)
```

```python
import functools

import jax
import jax.numpy as jnp
from jax import lax
from jax.experimental import pallas as pl
from jax.experimental.pallas import tpu as pltpu
from jax.sharding import PartitionSpec as P

MLPS = 3
BLK = 128
CHUNKS = 2
UNROLL = 28
LABEL_ROWS = 16
SPARE = 6
GRANT = 12 * 1024 * 1024

pair_scale = 0.7071067811865476


def split_bits(devices):
    count = devices.bit_length() - 1
    near = [bit for bit in (0, 2) if bit < count]
    far = [bit for bit in range(count) if bit not in near]
    return near, far


def xor_pairs(devices, mask):
    return [(i, i ^ mask) for i in range(devices)]


def near_mask(near, k):
    return sum(((k >> i) & 1) << bit for i, bit in enumerate(near))


def grant(extra=0):
    return pltpu.CompilerParams(vmem_limit_bytes=GRANT + extra)


def spent(microseconds):
    return pl.CostEstimate(
        flops=0, bytes_accessed=int(microseconds * 3.69e6), transcendentals=0
    )


def after_all(value, *others):
    if not others:
        return value
    return lax.optimization_barrier((value, *others))[0]


def full(shape):
    return pl.BlockSpec(memory_space=pltpu.VMEM)


def smem():
    return pl.BlockSpec(memory_space=pltpu.SMEM)


def pack_kernel(near, far, room, rows, blocks, owner, source, target, counts, basis, *refs):
    groups = 1 << len(near)
    whole, cut = refs[: groups - 1], refs[groups - 1 : groups - 1 + CHUNKS]
    table, fill = refs[groups - 1 + CHUNKS :]
    slots = basis.shape[0]
    me = lax.axis_index("graph")
    core = lax.axis_index("mp")
    for k in range(groups):
        fill[k] = 0

    def clear(i, carry):
        table[i] = -1
        return carry

    lax.fori_loop(0, groups * room, clear, 0, unroll=4)

    def route(t, carry):
        rel = owner[t] ^ me
        k = 0
        for i, bit in enumerate(near):
            k = k + (((rel >> bit) & 1) << i)
        p = fill[k]
        fill[k] = p + 1
        table[k * room + p] = t
        return carry

    lax.fori_loop(0, slots, route, 0)

    share = rows * CHUNKS
    first = core * share
    row = lax.broadcasted_iota(jnp.int32, (share, BLK), 0)
    label_row = lax.broadcasted_iota(jnp.int32, (LABEL_ROWS, BLK), 0)
    lane = lax.broadcasted_iota(jnp.int32, (LABEL_ROWS, BLK), 1)
    for k in range(groups):

        def one(p, labels):
            t = table[k * room + p]
            there = t >= 0
            s = jnp.maximum(t, 0)
            rel = owner[s] ^ me
            b = 0
            for i, bit in enumerate(far):
                b = b + (((rel >> bit) & 1) << (len(far) - 1 - i))
            place = jnp.where(there, b * blocks + target[s], 0)
            place = jnp.where(label_row == 0, place, source[s])
            labels = jnp.where(lane == p, place, labels)
            count = jnp.where(there, counts[s], 0)
            block = basis[s, pl.ds(pl.multiple_of(first, share), share), :]
            block = jnp.where(row + first < count, block, jnp.zeros_like(block))
            if k < groups - 1:
                whole[k][pl.ds(pl.multiple_of(p * share, share), share), :] = block
            else:
                for j in range(CHUNKS):
                    at = pl.ds(pl.multiple_of(p * rows, rows), rows)
                    cut[j][at, :] = block[j * rows : (j + 1) * rows]
            return labels

        labels = lax.fori_loop(0, room, one, jnp.zeros((LABEL_ROWS, BLK), jnp.int32), unroll=2)
        labels = labels.astype(jnp.float32).astype(jnp.bfloat16)
        if k < groups - 1:
            whole[k][room * share :, :] = labels
        else:
            cut[0][room * rows :, :] = labels


def add_products(room, height, labels, basis, mine, other, acc, staged, metas, sem):
    sources = len(basis)
    core = lax.axis_index("mp")
    width = mine[0].shape[1]
    own_cols = pl.ds(pl.multiple_of(core * width, width), width)
    other_cols = pl.ds(pl.multiple_of((1 - core) * width, width), width)
    for k in range(sources):
        staged[k] = labels[k][room * height :, :].astype(jnp.float32).astype(jnp.int32)[:8]
    copy = pltpu.make_async_copy(staged, metas, sem)
    copy.start()
    acc[...] = jnp.zeros_like(acc)
    copy.wait()
    for k in range(sources):

        def some(step, carry):
            sums = []
            for u in range(UNROLL):
                p = step * UNROLL + u
                s = metas[k, 1, p]
                at = pl.ds(pl.multiple_of(s * BLK, BLK), BLK)
                left = basis[k][pl.ds(pl.multiple_of(p * height, height), height), :]
                a = jnp.dot(left, mine[k][at, :], preferred_element_type=jnp.float32)
                b = jnp.dot(left, other[k][at, :], preferred_element_type=jnp.float32)
                sums.append((metas[k, 0, p], a, b))
            for at, a, b in sums:
                acc[at, :, own_cols] += a
                acc[at, :, other_cols] += b
            return carry

        lax.fori_loop(0, room // UNROLL, some, 0)


def first_kernel(sources, room, *refs):
    basis, mine, other = (refs[i * sources : (i + 1) * sources] for i in range(3))
    acc, staged, metas, sem = refs[3 * sources :]
    height = (basis[0].shape[0] - LABEL_ROWS) // room
    add_products(room, height, basis, basis, mine, other, acc, staged, metas, sem)


def last_kernel(room, blocks, rows, chunk, labels, basis, mine, other, before, *refs):
    keep_low, keep_high, send_low, send_high, acc, staged, metas, sem = refs
    held = slice(chunk * rows, (chunk + 1) * rows)
    add_products(room, rows, [labels], [basis], [mine], [other], acc, staged, metas, sem)
    part = keep_low.shape[0]
    for i, out in enumerate((keep_low, keep_high, send_low, send_high)):
        for o in range(part):
            at = slice((i * part + o) * blocks, (i * part + o + 1) * blocks)
            out[o] = (before[at, held] + acc[at]).astype(out.dtype)


def combine_kernel(rows, border, start, bases, *refs):
    mine, other = refs[:2]
    counts = [len(each) for each in bases]
    addends, outs = refs[2 : 2 + sum(counts)], refs[2 + sum(counts) :]
    combined, sends = outs[0], outs[1:]
    core = lax.axis_index("mp")
    width = mine.shape[1]
    own_cols = pl.ds(pl.multiple_of(core * width, width), width)
    other_cols = pl.ds(pl.multiple_of((1 - core) * width, width), width)
    for chunk in range(CHUNKS):
        parts = addends[sum(counts[:chunk]) : sum(counts[: chunk + 1])]
        first = core * (rows * CHUNKS) + chunk * rows
        held_rows = slice(chunk * rows, (chunk + 1) * rows)
        for i in range(combined.shape[0]):
            b = start + i
            at = pl.ds(pl.multiple_of(b * BLK + first, rows), rows)
            for cols, held in ((own_cols, mine), (other_cols, other)):
                total = held[at, :].astype(jnp.float32)
                for part, base in zip(parts, bases[chunk]):
                    total = total + part[0, b - base, :, cols].astype(jnp.float32)
                combined[i, held_rows, cols] = total.astype(combined.dtype)
    if sends:
        odd = lax.axis_index("graph") % 2
        even_send, odd_send = sends
        even_send[...] = combined[pl.ds((1 - odd) * border, border)]
        odd_send[...] = combined[pl.ds(odd * border, border)]


def mlp_kernel(border, start, blocks, reverse, valid, combined, *refs):
    came, refs = (refs[:2], refs[2:]) if start == 0 else (None, refs)
    in_own, in_other, out_own, out_other, final_own, final_other, state = refs
    count, share, width = combined.shape
    core = lax.axis_index("mp")
    odd = lax.axis_index("graph") % 2 == 1
    first = core * share
    for i in range(count):
        b = start + i
        within = reverse[b] % blocks
        if came is None:
            pair = combined[jnp.clip(within - start, 0, count - 1)]
        else:
            w = jnp.clip(within - (border if b < border else 0), 0, border - 1)
            pair = jnp.where(odd == (b < border), came[0][w], came[1][w])
        state[i * share : (i + 1) * share] = (
            combined[i].astype(jnp.float32) + pair.astype(jnp.float32)
        ) * pair_scale
    for layer in range(MLPS):
        layer_input = state[...].astype(jnp.bfloat16)
        total = state[...]
        values = [
            jnp.dot(layer_input, w_in[layer], preferred_element_type=jnp.float32)
            for w_in in (in_own, in_other)
        ]
        hidden = [(0.5 * v * (1.0 + jnp.tanh(0.5 * v))).astype(jnp.bfloat16) for v in values]
        for part, w_out in zip(hidden, (out_own, out_other)):
            total = total + jnp.dot(part, w_out[layer], preferred_element_type=jnp.float32)
        state[...] = total
    half = width // 2
    own_cols = pl.ds(pl.multiple_of(core * half, half), half)
    other_cols = pl.ds(pl.multiple_of((1 - core) * half, half), half)
    row = lax.broadcasted_iota(jnp.int32, (share, half), 0) + first
    limit = valid[0]
    for i in range(count):
        keep = row + (start + i) * BLK < limit
        at = slice(i * share, (i + 1) * share)
        final_own[i] = jnp.where(keep, state[at, own_cols], 0.0).astype(final_own.dtype)
        final_other[i] = jnp.where(keep, state[at, other_cols], 0.0).astype(final_other.dtype)


def join_kernel(starts, *refs):
    parts = len(starts)
    own, came, out = refs[:parts], refs[parts : 2 * parts], refs[2 * parts]
    core = lax.axis_index("mp")
    for i, start in enumerate(starts):
        count, share, _ = own[i].shape
        for b in range(count):
            here = (start + b) * BLK + core * share
            there = (start + b) * BLK + (1 - core) * share
            out[pl.ds(pl.multiple_of(here, share), share), :] = own[i][b]
            out[pl.ds(pl.multiple_of(there, share), share), :] = came[i][b]


def local(
    messages,
    basis_blocks,
    source_block,
    target_owner,
    target_block,
    row_counts,
    reverse_block,
    valid_edges,
    weight_in,
    weight_out,
):
    devices = lax.axis_size("graph")
    edge_rows, part_width = messages.shape
    width = part_width * lax.axis_size("mp")
    blocks = edge_rows // BLK
    slots = source_block.shape[0]
    capacity = max(2, (slots + devices - 1) // devices + 1)
    border = blocks // 4
    near, far = split_bits(devices)
    groups = 1 << len(near)
    owners = devices // groups
    room = min(slots, capacity * owners)
    room = -(-room // UNROLL) * UNROLL
    rows = BLK // lax.axis_size("mp") // CHUNKS
    bf16 = jnp.bfloat16

    def near_send(array, k):
        return lax.ppermute(array, "graph", xor_pairs(devices, near_mask(near, k)))

    def far_send(array, bit):
        return lax.ppermute(array, "graph", xor_pairs(devices, 1 << bit))

    def swap(array):
        return lax.ppermute(array, "mp", [(0, 1), (1, 0)])

    mine = [messages, near_send(messages, 1), near_send(messages, 2)]
    in_other, out_other = swap(weight_in), swap(weight_out)

    share = rows * CHUNKS
    whole_shape = jax.ShapeDtypeStruct((room * share + LABEL_ROWS, BLK), bf16)
    cut_shapes = [
        jax.ShapeDtypeStruct((room * rows + (LABEL_ROWS if j == 0 else SPARE * rows), BLK), bf16)
        for j in range(CHUNKS)
    ]
    packed = pl.pallas_call(
        functools.partial(pack_kernel, near, far, room, rows, blocks),
        out_shape=[whole_shape] * (groups - 1) + cut_shapes,
        in_specs=[smem()] * 4 + [full(None)],
        out_specs=[full(None)] * (groups - 1 + CHUNKS),
        scratch_shapes=[pltpu.SMEM((groups * room,), jnp.int32), pltpu.SMEM((groups,), jnp.int32)],
        compiler_params=grant(),
        cost_estimate=spent(6),
        name="pack",
    )(
        target_owner[:, 0],
        source_block,
        target_block,
        row_counts,
        after_all(basis_blocks, in_other, out_other),
    )
    last = groups - 1
    middle = edge_rows // 2
    other = [swap(after_all(messages, packed[0]))]
    basis = [packed[0]]
    for k in range(1, last):
        basis.append(near_send(packed[k], k))
    ready = [after_all(array, packed[0]) for array in mine[1:]]
    onward = [near_send(ready[0][:middle], 2), near_send(ready[1][middle:], 1)]
    mine.append(jnp.concatenate(onward, axis=0))
    other.extend(swap(after_all(array, *basis[1:])) for array in mine[1:])
    acc_shape = (owners * blocks, rows, width)
    acc_bytes = owners * blocks * rows * width * 4
    partial = pl.pallas_call(
        functools.partial(first_kernel, last, room),
        out_shape=jax.ShapeDtypeStruct((owners * blocks, share, width), jnp.float32),
        in_specs=[full(None)] * (3 * last),
        out_specs=full(None),
        scratch_shapes=[
            pltpu.VMEM((last, 8, BLK), jnp.int32),
            pltpu.SMEM((last, 8, BLK), jnp.int32),
            pltpu.SemaphoreType.DMA,
        ],
        compiler_params=grant(CHUNKS * acc_bytes),
        cost_estimate=spent(4),
        name="first_products",
    )(*basis[:last], *mine[:last], *other[:last])

    part_owners_shape = jax.ShapeDtypeStruct((owners // 4, blocks, rows, width), bf16)
    border_shape = jax.ShapeDtypeStruct((border, share, width), bf16)
    even_pairs = [(i, i ^ 1) for i in range(devices)]
    odd_pairs = [(i, (i + 1 if i % 2 else i - 1) % devices) for i in range(devices)]
    cut, waited = [], basis[1:]
    sums, lows, highs = [], [], []
    for chunk in range(CHUNKS):
        cut.append(near_send(after_all(packed[last + chunk], *waited), last))
        keep_low, keep_high, send_low, send_high = pl.pallas_call(
            functools.partial(last_kernel, room, blocks, rows, chunk),
            out_shape=[part_owners_shape] * 4,
            in_specs=[full(None)] * 5,
            out_specs=[full(None)] * 4,
            scratch_shapes=[
                pltpu.VMEM(acc_shape, jnp.float32),
                pltpu.VMEM((1, 8, BLK), jnp.int32),
                pltpu.SMEM((1, 8, BLK), jnp.int32),
                pltpu.SemaphoreType.DMA,
            ],
            compiler_params=grant(4 * acc_bytes),
            cost_estimate=spent(2),
            name="last_products",
        )(cut[0], cut[chunk], mine[last], other[last], partial)
        waited = [partial]
        came = far_send(send_high, far[0])
        sums.append((keep_high.astype(jnp.float32) + came.astype(jnp.float32)).astype(bf16))
        highs.append(came)
        lows.append((keep_low, send_low))
    lows = [
        (keep_low, far_send(after_all(send_low, highs[-1]), far[0]))
        for keep_low, send_low in lows
    ]
    starts = [0, 2 * border]
    stops = [2 * border, blocks]
    arrived = []
    for chunk in range(CHUNKS):
        pieces = [(0, blocks)] if chunk < CHUNKS - 1 else list(zip(starts, stops))
        found = []
        for start, stop in pieces:
            send, addends, bases = sums[chunk][:, start:stop], list(lows[chunk]), [0, 0]
            if start > 0:
                send = after_all(send, arrived[0][0][0][-1])
            size = owners // 4
            for index, bit in enumerate(far[1:]):
                addends.append(far_send(send, bit))
                bases.append(start)
                if index + 2 < len(far):
                    size = size // 2
                    send = sum(
                        part[size : 2 * size, start - base : stop - base].astype(jnp.float32)
                        for part, base in zip(addends, bases)
                    ).astype(bf16)
            found.append((addends, tuple(bases)))
        arrived.append(found if len(found) > 1 else found * 2)
    finals, came = [], []
    for index, (start, stop) in enumerate(zip(starts, stops)):
        addends = [array for found in arrived for array in found[index][0]]
        bases = tuple(found[index][1] for found in arrived)
        piece_shape = jax.ShapeDtypeStruct((stop - start, share, width), bf16)
        part_shape = jax.ShapeDtypeStruct((stop - start, share, part_width), bf16)
        outs = pl.pallas_call(
            functools.partial(combine_kernel, rows, border, start, bases),
            out_shape=[piece_shape] + [border_shape] * (2 if start == 0 else 0),
            in_specs=[full(None)] * (2 + len(addends)),
            out_specs=[full(None)] * (3 if start == 0 else 1),
            compiler_params=grant(acc_bytes),
            cost_estimate=spent(0.5),
            name="combine",
        )(mine[0], other[0], *addends)
        if start == 0:
            came = [
                lax.ppermute(outs[2], "graph", odd_pairs),
                lax.ppermute(outs[1], "graph", even_pairs),
            ][::-1]
        operands = [outs[0]] + (came if start == 0 else [])
        own, theirs = pl.pallas_call(
            functools.partial(mlp_kernel, border, start, blocks),
            out_shape=[part_shape] * 2,
            in_specs=[smem()] * 2 + [full(None)] * (4 + len(operands)),
            out_specs=[full(None)] * 2,
            scratch_shapes=[pltpu.VMEM(((stop - start) * share, width), jnp.float32)],
            compiler_params=grant(),
            cost_estimate=spent(2),
            name="mlp",
        )(reverse_block, valid_edges, *operands, weight_in, in_other, weight_out, out_other)
        finals.append((own, swap(theirs)))

    return pl.pallas_call(
        functools.partial(join_kernel, starts),
        out_shape=jax.ShapeDtypeStruct(messages.shape, bf16),
        in_specs=[full(None)] * (2 * len(finals)),
        out_specs=full(None),
        compiler_params=grant(),
        cost_estimate=spent(1),
        name="join",
    )(*[own for own, _ in finals], *[theirs for _, theirs in finals])


def solution(mesh):
    in_specs = (
        P("graph", "mp"),
        P("graph", None, None),
        P("graph"),
        P("graph", None),
        P("graph"),
        P("graph"),
        P("graph"),
        P("graph"),
        P(None, None, "mp"),
        P(None, "mp", None),
    )
    out_specs = P("graph", "mp")
    return jax.shard_map(local, mesh=mesh, in_specs=in_specs, out_specs=out_specs, check_vma=False)
```
